512 devices in a mesh: space: 32 (over x, z), probe: 16 (over y, core).
Axes of the slice: x: 4, y: 8, z: 8, core: 2. Of those that a mesh axis runs over, the one named last changes fastest.
Arguments:
- conductivity: float32 [256, 8192], P('space'), may hold values from 1 to 2
- leakage: float32 [256, 8192], P('space'), may hold values from 0.005 to 0.05
- signs: int32 [64, 256], P('probe'), may hold values from 0 to 1
- wells: int32 [256], replicated, may hold values from 0 to 2097151
Outputs:
- basis: float32 [64, 2097152], P(None, ('space', 'probe'))
- factor: float32 [64, 64], replicated
The draws below stay inside these ranges and needn't reach their ends.
Inputs may be any that keep to these rules, and one draw needn't show every extreme that they name: Probe k gives well w the sign 2 signs[k, w] - 1. Flat cell indices; wells may repeat.
All inputs are finite; a program needn't handle non-finite values.
Results may differ from the reference program's by a relative error of at most 0.0003.
Values sent between devices are 32-bit elements; how exact they have to be, the bound alone decides.
A program may use at most 128 MiB of HBM per device.

```python
import math
import jax
import jax.numpy as jnp
from jax import lax

NY = 128
NZ = 64
PROBES = 64
WELLS = 256
SWEEPS = 16
NX = 256


def draw_conductivity(key, part):
    key = jax.random.fold_in(key, 11)
    level = jax.random.uniform(key, (NX, NY * NZ), jnp.float32)
    power = level ** 4
    return 2.0 * jnp.exp(-math.log(2.0) * power)


def touch_ends(values, stream_key, least, high):
    shape = values.shape
    spot = [jax.random.randint(jax.random.fold_in(stream_key, axis), (), 0, shape[axis]) for axis in range(len(shape))]
    values = values.at[tuple(spot)].set(least)
    longest = shape.index(max(shape))
    spot[longest] = (spot[longest] + 1) % shape[longest]
    return values.at[tuple(spot)].set(high)


def levels(own_key, extent, cuts, smallest, largest):
    gain = 1.0
    for dim, parts in cuts:
        heights = jax.random.uniform(jax.random.fold_in(jax.random.fold_in(own_key, 6), dim), (parts,), jnp.float32, smallest / len(cuts), largest / len(cuts))
        gain = gain * jnp.repeat(jnp.exp(heights), extent[dim] // parts).reshape((-1,) + (1,) * (len(extent) - 1 - dim))
    return gain


def setup_inputs(seed: int = 0) -> dict:
    key_of = jax.random.split(jax.random.key(seed), 5)
    conductivity = draw_conductivity(jax.random.fold_in(key_of[4], 71), 0)
    leakage = jnp.clip(jnp.exp(math.log(0.05) - 2.3025851 * jax.random.uniform(key_of[1], (NX, NY * NZ), jnp.float32) ** levels(key_of[1], (NX, NY * NZ), ((0, 32),), -0.2, 0.2)), 0.005, 0.05)
    signs = touch_ends(jax.random.randint(key_of[2], (PROBES, WELLS), 0, 2), jax.random.fold_in(key_of[2], 1), 0, 1).astype(jnp.int32)
    wells = touch_ends(jax.random.randint(key_of[3], (WELLS,), 0, NX * NY * NZ), jax.random.fold_in(key_of[3], 1), 0, (NX * NY * NZ) - 1).astype(jnp.int32)
    return dict(conductivity=conductivity, leakage=leakage, signs=signs, wells=wells)


bound_low = 0.005
bound_high = 24.5

def chebyshev_table(count):
    center = 0.5 * (bound_high + bound_low)
    spread = 0.5 * (bound_high - bound_low)
    ratio = center / spread
    rho_prev = 1.0 / ratio
    entries = []
    for index_step in range(count):
        rho_next = 1.0 / (2.0 * ratio - rho_prev)
        entries.append([rho_next * rho_prev, 2.0 * rho_next / spread])
        rho_prev = rho_next
    return jnp.array(entries, dtype=jnp.float32)

def start_scale():
    return 1.0 / (0.5 * (bound_high + bound_low))

def reference(conductivity, leakage, signs, wells):
    cube = conductivity.reshape(NX, NY, NZ)
    leak_cube = leakage.reshape(NX, NY, NZ)
    padded = jnp.pad(cube, 1, mode='edge')
    faces = (leak_cube, 0.5 * (cube + padded[:-2, 1:-1, 1:-1]), 0.5 * (cube + padded[2:, 1:-1, 1:-1]), 0.5 * (cube + padded[1:-1, :-2, 1:-1]), 0.5 * (cube + padded[1:-1, 2:, 1:-1]), 0.5 * (cube + padded[1:-1, 1:-1, :-2]), 0.5 * (cube + padded[1:-1, 1:-1, 2:]))

    def operate(field):
        outer = jnp.pad(field, 1)
        result = faces[0] * field + faces[1] * (field - outer[:-2, 1:-1, 1:-1])
        result = result + faces[2] * (field - outer[2:, 1:-1, 1:-1])
        result = result + faces[3] * (field - outer[1:-1, :-2, 1:-1])
        result = result + faces[4] * (field - outer[1:-1, 2:, 1:-1])
        result = result + faces[5] * (field - outer[1:-1, 1:-1, :-2])
        result = result + faces[6] * (field - outer[1:-1, 1:-1, 2:])
        return result
    table = chebyshev_table(SWEEPS)
    weights = (2 * signs - 1).astype(jnp.float32)
    sources = jnp.zeros((PROBES, NX * NY * NZ), jnp.float32).at[:, wells].add(weights)

    def solve_one(source):
        field = source.reshape(NX, NY, NZ)

        def sweep(step, carry):
            iterate, resid, search = carry
            image = operate(search)
            iterate = iterate + search
            resid = resid - image
            search = table[step, 0] * search + table[step, 1] * resid
            return (iterate, resid, search)
        start = (jnp.zeros_like(field), field, field * start_scale())
        final = lax.fori_loop(0, SWEEPS, sweep, start)
        return final[0].reshape(-1)
    sketch = lax.map(solve_one, sources)
    gram = jnp.dot(sketch.astype(jnp.float32), sketch.T.astype(jnp.float32), precision=lax.Precision.HIGHEST, preferred_element_type=jnp.float32)
    lower = jnp.linalg.cholesky(gram)
    basis = jax.scipy.linalg.solve_triangular(lower, sketch, lower=True) * math.sqrt(NX * NY * NZ)
    factor = lower.T / math.sqrt(WELLS)
    return (basis, factor)
```

```python
import functools
import math

import jax
import jax.numpy as jnp
from jax import lax
from jax.experimental import pallas as pl
from jax.experimental.pallas import tpu as pltpu
from jax.sharding import PartitionSpec as P

NZ = 64
SWEEPS = 16
REACH = 2
SPAN = 2 * REACH + 1
GROUP = 16
CHIPS = 8
SLOTS = GROUP * SPAN
QUADS = 8
PAIRS = 32
PAD = 16

bound_low = 0.005
bound_high = 24.5

F32 = jnp.float32
VMEM = pltpu.VMEM
SMEM = pltpu.SMEM


def chebyshev_table(count):
    center = 0.5 * (bound_high + bound_low)
    spread = 0.5 * (bound_high - bound_low)
    ratio = center / spread
    rho_prev = 1.0 / ratio
    entries = []
    for index_step in range(count):
        rho_next = 1.0 / (2.0 * ratio - rho_prev)
        entries.append((rho_next * rho_prev, 2.0 * rho_next / spread))
        rho_prev = rho_next
    return entries


def start_scale():
    return 1.0 / (0.5 * (bound_high + bound_low))


def decode(cell):
    cell = jnp.maximum(cell, 0)
    x = lax.shift_right_logical(cell, 13)
    y = lax.bitwise_and(lax.shift_right_logical(cell, 6), 127)
    z = lax.bitwise_and(cell, 63)
    y_first = lax.bitwise_and(y + 1, 126 + 128) - 16
    return x, y, y_first, z, z - 15


def lanes(shape=(8, 128)):
    return lax.broadcasted_iota(jnp.int32, shape, 1)


def sublanes(shape=(8, 128)):
    return lax.broadcasted_iota(jnp.int32, shape, 0)


def wrap(shift):
    return lax.bitwise_and(shift, 127)


def cut_kernel(cell_ref, cond_ref, leak_ref, out_ref):
    me = lax.axis_index("probe")
    chip = me // 2
    core = me % 2
    lane = lanes()
    for e in range(SPAN):
        _, _, y_first, _, z_first = decode(cell_ref[core, chip * SPAN + e])
        pair_first = y_first // 2
        shifts = [wrap(128 - z_first), wrap(96 - z_first), wrap(64 - z_first + 128), wrap(32 - z_first + 128)]
        for k in range(QUADS):
            one = pl.multiple_of(jnp.clip(pair_first + 2 * k, 0, 63) * 128, 128)
            two = pl.multiple_of(jnp.clip(pair_first + 2 * k + 1, 0, 63) * 128, 128)
            for prop, ref in enumerate((cond_ref, leak_ref)):
                a = ref[:, pl.ds(one, 128)]
                b = ref[:, pl.ds(two, 128)]
                low = jnp.where(lane < 32, pltpu.roll(a, shifts[0], 1), pltpu.roll(a, shifts[1], 1))
                high = jnp.where(lane < 96, pltpu.roll(b, shifts[2], 1), pltpu.roll(b, shifts[3], 1))
                out_ref[e, prop, k] = jnp.where(lane < 64, low, high)


def barrier_with(partners):
    barrier = pltpu.get_barrier_semaphore()
    for partner in partners:
        pl.semaphore_signal(barrier, inc=1, device_id=partner, device_id_type=pl.DeviceIdType.MESH)
    pl.semaphore_wait(barrier, len(partners))


def remote(src, dst, send, recv, device):
    return pltpu.make_async_remote_copy(
        src_ref=src, dst_ref=dst, send_sem=send, recv_sem=recv, device_id=device, device_id_type=pl.DeviceIdType.MESH
    )


OFFSETS = (-2, -1, 1, 2)


def window_kernel(own_ref, signs_ref, win_ref, sign_out, send_sem, recv_sem, sign_send, sign_recv, pair_sem):
    count = lax.axis_size("space")
    here = lax.axis_index("space")
    me = lax.axis_index("probe")
    chip = me // 2
    core = me % 2
    near = [(lax.rem(here + d + count, count), me) for d in OFFSETS]
    along = [(here, lax.rem(chip + r, CHIPS) * 2 + core) for r in range(1, CHIPS)]
    twin = (here, chip * 2 + 1 - core)
    barrier_with(near + along + [twin])
    copies = []
    for i, d in enumerate(OFFSETS):
        copies.append(remote(own_ref.at[d + 2], win_ref.at[2 - d], send_sem.at[i], recv_sem.at[i], near[i]))
        copies[-1].start()
    signs = []
    for r in range(1, CHIPS):
        signs.append(remote(signs_ref, sign_out.at[core, chip], sign_send.at[r], sign_recv.at[r], along[r - 1]))
        signs[-1].start()
    win_ref[REACH] = own_ref[REACH]
    sign_out[core, chip] = signs_ref[...]
    for copy in signs:
        copy.wait()
    pair = remote(sign_out.at[core], sign_out.at[core], pair_sem.at[0], pair_sem.at[1], twin)
    pair.start()
    pair.wait()
    for copy in copies:
        copy.wait()


def shifted(own, before, after, lane_group, sub):
    down = pltpu.roll(own, 1, 0)
    up = pltpu.roll(own, 7, 0)
    return down, up


def solve_kernel(cell_ref, win_ref, out_ref, coef, search, resid, total):
    here = lax.axis_index("space")
    me = lax.axis_index("probe")
    chip = me // 2
    core = me % 2
    cell = cell_ref[core, chip * SPAN + REACH]
    x, y, y_first, z, z_first = decode(cell)
    lane = lanes()
    sub = sublanes()
    group = lane // 32
    depth = lane % 32
    zz = z_first + depth
    z_ok = (zz >= 0) & (zz < NZ)
    zm_ok = z_ok & (zz >= 1)
    zp_ok = z_ok & (zz < NZ - 1)
    weight = jnp.where(cell >= 0, 1.0, 0.0).astype(F32)

    for b in range(SPAN):
        xx = (here + (b - REACH)) * 8 + sub
        x_ok = (xx >= 0) & (xx < 256)
        xm_in = xx >= 1
        xp_in = xx < 255
        for k in range(QUADS):
            yy = y_first + 4 * k + group
            y_ok = (yy >= 0) & (yy < 128)
            inside = x_ok & y_ok & z_ok
            own = win_ref[b, 0, k]
            before = win_ref[max(b - 1, 0), 0, k]
            after = win_ref[min(b + 1, SPAN - 1), 0, k]
            left = win_ref[b, 0, max(k - 1, 0)]
            right = win_ref[b, 0, min(k + 1, QUADS - 1)]
            parts = (
                (jnp.where(sub == 0, pltpu.roll(before, 1, 0), pltpu.roll(own, 1, 0)), xm_in),
                (jnp.where(sub == 7, pltpu.roll(after, 7, 0), pltpu.roll(own, 7, 0)), xp_in),
                (jnp.where(group == 0, pltpu.roll(left, 32, 1), pltpu.roll(own, 32, 1)), yy >= 1),
                (jnp.where(group == 3, pltpu.roll(right, 96, 1), pltpu.roll(own, 96, 1)), yy < 127),
                (pltpu.roll(own, 1, 1), zz >= 1),
                (pltpu.roll(own, 127, 1), zz < NZ - 1),
            )
            diagonal = win_ref[b, 1, k]
            for n, (other, there) in enumerate(parts):
                face = 0.5 * (own + jnp.where(there, other, own))
                diagonal = diagonal + face
                coef[n + 1, b, k] = jnp.where(inside & there, face, 0.0)
            coef[0, b, k] = diagonal

    zero = jnp.zeros((8, 128), F32)
    x_in = x - here * 8
    for b in range(SPAN):
        for k in range(QUADS):
            search[1, b, k] = zero
            if b == REACH and k in (3, 4):
                hit = (sub == x_in) & (4 * k + group == y - y_first) & (depth == 15)
                source = jnp.where(hit, weight, 0.0)
                resid[b, k] = source
                search[0, b, k] = source * start_scale()
            else:
                resid[b, k] = zero
                search[0, b, k] = zero
            total[b, k] = zero

    table = chebyshev_table(SWEEPS)
    for j in range(SWEEPS - 1):
        a, c = (float(value) for value in table[j])
        now, later = j % 2, (j + 1) % 2
        wide = j + 1
        k_low, k_high = (15 - wide) // 4, (16 + wide) // 4
        b_low, b_high = (1, 3) if wide <= 8 else (0, 4)
        for b in range(b_low, b_high + 1):
            for k in range(k_low, k_high + 1):
                own = search[now, b, k]
                down = pltpu.roll(own, 1, 0)
                up = pltpu.roll(own, 7, 0)
                edge = pltpu.roll(search[now, b - 1, k], 1, 0) if b > 0 else zero
                down = jnp.where(sub == 0, edge, down)
                edge = pltpu.roll(search[now, b + 1, k], 7, 0) if b < SPAN - 1 else zero
                up = jnp.where(sub == 7, edge, up)
                edge = pltpu.roll(search[now, b, k - 1], 32, 1) if k > 0 else zero
                left = jnp.where(group == 0, edge, pltpu.roll(own, 32, 1))
                edge = pltpu.roll(search[now, b, k + 1], 96, 1) if k < QUADS - 1 else zero
                right = jnp.where(group == 3, edge, pltpu.roll(own, 96, 1))
                image = coef[0, b, k] * own
                image = image - coef[1, b, k] * down
                image = image - coef[2, b, k] * up
                image = image - coef[3, b, k] * left
                image = image - coef[4, b, k] * right
                image = image - coef[5, b, k] * pltpu.roll(own, 1, 1)
                image = image - coef[6, b, k] * pltpu.roll(own, 127, 1)
                rest = resid[b, k] - image
                resid[b, k] = rest
                total[b, k] = total[b, k] + own
                search[later, b, k] = a * own + c * rest
    last = (SWEEPS - 1) % 2
    for b in range(SPAN):
        for k in range(QUADS):
            total[b, k] = total[b, k] + search[last, b, k]
    for b in range(SPAN):
        for r in range(8):
            out_ref[b, r] = total[b, :, r, :]


def spread_kernel(own_ref, out_ref, block_ref, send_sem, recv_sem, row_send, row_recv, pair_send, pair_recv):
    count = lax.axis_size("space")
    here = lax.axis_index("space")
    me = lax.axis_index("probe")
    chip = me // 2
    core = me % 2
    near = [(lax.rem(here + d + count, count), me) for d in OFFSETS]
    along = [(here, lax.rem(chip + r, CHIPS) * 2 + core) for r in range(1, CHIPS)]
    twin = (here, chip * 2 + 1 - core)
    barrier_with(near + along + [twin])
    copies = []
    for i, d in enumerate(OFFSETS):
        copies.append(remote(own_ref.at[d + 2], block_ref.at[2 - d], send_sem.at[i], recv_sem.at[i], near[i]))
        copies[-1].start()
    block_ref[REACH] = own_ref[REACH]
    for copy in copies:
        copy.wait()
    rows = []
    for r in range(1, CHIPS):
        target = lax.rem(chip + r, CHIPS)
        rows.append(
            remote(block_ref.at[:, target], out_ref.at[core, chip], row_send.at[r], row_recv.at[r], along[r - 1])
        )
        rows[-1].start()
    out_ref[core, chip] = block_ref[:, chip]
    pairs = []
    for r in range(CHIPS):
        source = lax.rem(chip - r + CHIPS, CHIPS)
        if r:
            rows[r - 1].wait_recv()
        part = out_ref.at[core, source]
        pairs.append(remote(part, part, pair_send.at[r], pair_recv.at[r], twin))
        pairs[-1].start()
    for copy in rows:
        copy.wait_send()
    for copy in pairs:
        copy.wait()


def split3(value):
    high = value.astype(jnp.bfloat16)
    rest = value - high.astype(F32)
    mid = rest.astype(jnp.bfloat16)
    low = (rest - mid.astype(F32)).astype(jnp.bfloat16)
    return high, mid, low


def place_kernel(turn_ref, cell_ref, part_ref, slot_ref, signs_ref, before_ref, out_ref, gram_ref, placed):
    half = lax.axis_index("probe") % 2
    lane = lanes()

    def clear(i, _):
        placed[pl.ds(pl.multiple_of(i * 64, 64), 64), :] = jnp.zeros((64, 128), F32)
        return 0

    lax.fori_loop(0, (PAIRS + 2 * PAD) * SLOTS // 64, clear, 0)

    def place(n, _):
        for c in range(2):
            _, _, y_first, _, z_first = decode(cell_ref[c, n])
            first = jnp.clip(y_first // 2 - PAIRS * half, -PAD, PAIRS) + PAD
            own = part_ref[c, n]
            shift = lane - z_first
            even = (shift >= 0) & (shift < 32) & (lane < 64)
            odd = (shift >= 64) & (shift < 96) & (lane >= 64)
            for m in range(2):
                row = jnp.where(even, pltpu.roll(own, wrap(z_first - 64 * m + 256), 1), 0.0)
                row = jnp.where(odd, pltpu.roll(own, wrap(z_first + 32 - 64 * m + 256), 1), row)
                start = (first + m) * SLOTS + c * (SLOTS // 2) + n
                placed[pl.ds(start, 8, stride=2 * SLOTS), :] = row
        return 0

    lax.fori_loop(0, SLOTS // 2, place, 0)

    table = jnp.concatenate([signs_ref[p % 2, p // 2] for p in range(GROUP)], axis=0)
    table = (2 * table - 1).astype(jnp.bfloat16)
    which = lax.broadcasted_iota(jnp.int32, (256, 128), 0) == slot_ref[...]
    pick = jnp.dot(table, which.astype(jnp.bfloat16), preferred_element_type=F32)
    pick = pick[:, :SLOTS].astype(jnp.bfloat16)
    pick = jnp.concatenate([pick, pick, pick], axis=1)
    first_turn = turn_ref[0] == 0
    gram = jnp.zeros((64, 64), F32)
    for t in range(PAIRS):
        base = (t + PAD) * SLOTS
        value = jnp.concatenate(split3(placed[base : base + SLOTS, :]), axis=0)
        value = jnp.dot(pick, value, preferred_element_type=F32)
        value = value + jnp.where(first_turn, 0.0, before_ref[:, 128 * t : 128 * t + 128])
        out_ref[:, 128 * t : 128 * t + 128] = value
    sketch = out_ref[...]
    gram = lax.dot_general(
        sketch, sketch, (((1,), (1,)), ((), ())), precision=lax.Precision.HIGHEST, preferred_element_type=F32
    )
    gram = jnp.concatenate([gram, jnp.zeros((64, 64), F32)], axis=1)
    for p in range(GROUP):
        gram_ref[p] = gram[4 * p : 4 * p + 4]


def sum_kernel(part_ref, out_ref, got, z_buf, x_buf, s1, r1, s2, r2, s3, r3, s4, r4):
    here = lax.axis_index("space")
    me = lax.axis_index("probe")
    x = here // 8
    z = here % 8
    group = [(here, lax.rem(me + r, GROUP)) for r in range(1, GROUP)]
    ring_z = [(x * 8 + lax.rem(z + r, 8), me) for r in range(1, 8)]
    ring_x = [(lax.rem(x + r, 4) * 8 + z, me) for r in range(1, 4)]
    barrier_with(group + ring_z + ring_x)
    copies = []
    for r in range(1, GROUP):
        copies.append(remote(part_ref.at[lax.rem(me + r, GROUP)], got.at[r], s1.at[r], r1.at[r], group[r - 1]))
        copies[-1].start()
    value = part_ref[me]
    for r in range(1, GROUP):
        copies[r - 1].wait_recv()
    got[0] = value
    total = got[0]
    for r in range(1, GROUP):
        total = total + got[r]
    z_buf[z] = total
    steps = []
    for r in range(1, 8):
        steps.append(remote(z_buf.at[z], z_buf.at[z], s2.at[r], r2.at[r], ring_z[r - 1]))
        steps[-1].start()
    for copy in steps:
        copy.wait_recv()
    total = z_buf[0]
    for r in range(1, 8):
        total = total + z_buf[r]
    x_buf[x] = total
    turns = []
    for r in range(1, 4):
        turns.append(remote(x_buf.at[x], x_buf.at[x], s3.at[r], r3.at[r], ring_x[r - 1]))
        turns[-1].start()
    for copy in turns:
        copy.wait_recv()
    total = ((x_buf[0] + x_buf[1]) + x_buf[2]) + x_buf[3]
    out_ref[me] = total
    last = []
    for r in range(1, GROUP):
        last.append(remote(out_ref.at[me], out_ref.at[me], s4.at[r], r4.at[r], group[r - 1]))
        last[-1].start()
    for copy in copies + steps + turns:
        copy.wait_send()
    for copy in last:
        copy.wait()


def finish_kernel(gram_ref, sketch_ref, basis_ref, factor_ref):
    shape = (8, 128)
    lane = lanes(shape)
    sub = sublanes(shape)
    rows = []
    for i in range(8):
        block = jnp.concatenate([gram_ref[2 * i], gram_ref[2 * i + 1]], axis=0)
        rows.append(jnp.where(lane - 64 == sub + 8 * i, 1.0, block))
    for k in range(64):
        owner, inner = k // 8, k % 8
        row = jnp.broadcast_to(rows[owner][inner : inner + 1, :], shape)
        pivot = jnp.broadcast_to(row[:, k : k + 1], shape)
        scale = lax.rsqrt(pivot)
        scale = scale * (1.5 - 0.5 * pivot * scale * scale)
        row = row * scale
        for i in range(owner, 8):
            many = jnp.broadcast_to(rows[i][:, k : k + 1], shape) * scale
            fresh = rows[i] - many * row
            if i == owner:
                fresh = jnp.where(sub > inner, fresh, jnp.where(sub == inner, row, rows[i]))
            rows[i] = fresh
    full = jnp.concatenate(rows, axis=0)
    row_at = lax.broadcasted_iota(jnp.int32, (64, 64), 0)
    col_at = lax.broadcasted_iota(jnp.int32, (64, 64), 1)
    upper = jnp.where(col_at >= row_at, full[:, :64], 0.0)
    factor_ref[...] = upper * (1.0 / math.sqrt(256))
    inverse = full[:, 64:] * math.sqrt(256 * 128 * 64)
    basis_ref[...] = jnp.dot(
        inverse, sketch_ref[...], precision=lax.Precision.HIGHEST, preferred_element_type=F32
    )


def params(**more):
    return pltpu.CompilerParams(vmem_limit_bytes=48 * 1024 * 1024, **more)


def whole(space=VMEM):
    return pl.BlockSpec(memory_space=space)


def dma(*shape):
    return pltpu.SemaphoreType.DMA(shape)


def on_device(conductivity, leakage, signs, wells):
    here = lax.axis_index("space")
    cells = conductivity.shape[0] * conductivity.shape[1]
    probes = signs.shape[0] * GROUP
    count = wells.shape[0]
    owner = wells // cells
    index = jnp.arange(count, dtype=jnp.int32)
    rank = jnp.sum((owner[None, :] == owner[:, None]) & (index[None, :] < index[:, None]), axis=1, dtype=jnp.int32)
    rounds = jnp.max(rank) // GROUP + 1
    slot = jnp.arange(SLOTS, dtype=jnp.int32)
    slot_probe = (slot % (SLOTS // 2)) // SPAN * 2 + slot // (SLOTS // 2)
    slot_block = here + slot % SPAN - REACH

    def body(carry):
        turn, sketch, _ = carry
        match = (owner[None, :] == slot_block[:, None]) & (rank[None, :] == turn * GROUP + slot_probe[:, None])
        chosen = jnp.max(jnp.where(match, index[None, :], -1), axis=1)
        cell = jnp.max(jnp.where(match, wells[None, :], -1), axis=1).reshape(2, SLOTS // 2)
        chosen = jnp.concatenate([chosen, jnp.full((128 - SLOTS,), -1, jnp.int32)])[None, :]
        windows = pl.pallas_call(
            cut_kernel,
            out_shape=jax.ShapeDtypeStruct((SPAN, 2, QUADS, 8, 128), F32),
            in_specs=[whole(SMEM), whole(), whole()],
            out_specs=whole(),
            compiler_params=params(),
            name="cut",
        )(cell, conductivity, leakage)
        windows, all_signs = pl.pallas_call(
            window_kernel,
            out_shape=(
                jax.ShapeDtypeStruct((SPAN, 2, QUADS, 8, 128), F32),
                jax.ShapeDtypeStruct((2, CHIPS, probes // GROUP, count), jnp.int32),
            ),
            in_specs=[whole(), whole()],
            out_specs=(whole(), whole()),
            scratch_shapes=[dma(4), dma(4), dma(8), dma(8), dma(2)],
            compiler_params=params(collective_id=0, has_side_effects=True),
            name="windows",
        )(windows, signs)
        fields = pl.pallas_call(
            solve_kernel,
            out_shape=jax.ShapeDtypeStruct((SPAN, 8, QUADS, 128), F32),
            in_specs=[whole(SMEM), whole()],
            out_specs=whole(),
            scratch_shapes=[
                VMEM((7, SPAN, QUADS, 8, 128), F32),
                VMEM((2, SPAN, QUADS, 8, 128), F32),
                VMEM((SPAN, QUADS, 8, 128), F32),
                VMEM((SPAN, QUADS, 8, 128), F32),
            ],
            compiler_params=params(),
            name="solve",
        )(cell, windows)
        fields = pl.pallas_call(
            spread_kernel,
            out_shape=jax.ShapeDtypeStruct((2, CHIPS, SPAN, QUADS, 128), F32),
            in_specs=[whole()],
            out_specs=whole(),
            scratch_shapes=[VMEM((SPAN, 8, QUADS, 128), F32), dma(4), dma(4), dma(8), dma(8), dma(8), dma(8)],
            compiler_params=params(collective_id=1, has_side_effects=True),
            name="spread",
        )(fields)
        sketch, gram = pl.pallas_call(
            place_kernel,
            out_shape=(
                jax.ShapeDtypeStruct(sketch.shape, F32),
                jax.ShapeDtypeStruct((GROUP, 4, 128), F32),
            ),
            in_specs=[whole(SMEM), whole(SMEM), whole(), whole(), whole(), whole()],
            out_specs=(whole(), whole()),
            scratch_shapes=[VMEM(((PAIRS + 2 * PAD) * SLOTS, 128), F32)],
            compiler_params=params(),
            name="place",
        )(turn.reshape(1), cell, fields.reshape(2, SLOTS // 2, QUADS, 128), chosen, all_signs, sketch)
        return turn + 1, sketch, gram

    sketch = jnp.zeros((probes, cells // GROUP), F32)
    gram = jnp.zeros((GROUP, 4, 128), F32)
    _, sketch, gram = lax.while_loop(lambda carry: carry[0] < rounds, body, (jnp.int32(0), sketch, gram))
    gram = pl.pallas_call(
        sum_kernel,
        out_shape=jax.ShapeDtypeStruct((GROUP, 4, 128), F32),
        in_specs=[whole()],
        out_specs=whole(),
        scratch_shapes=[
            VMEM((GROUP, 4, 128), F32),
            VMEM((8, 4, 128), F32),
            VMEM((4, 4, 128), F32),
            dma(GROUP),
            dma(GROUP),
            dma(8),
            dma(8),
            dma(4),
            dma(4),
            dma(GROUP),
            dma(GROUP),
        ],
        compiler_params=params(collective_id=2, has_side_effects=True),
        name="gram_sum",
    )(gram)
    return pl.pallas_call(
        finish_kernel,
        out_shape=(
            jax.ShapeDtypeStruct((probes, cells // GROUP), F32),
            jax.ShapeDtypeStruct((probes, probes), F32),
        ),
        in_specs=[whole(), whole()],
        out_specs=(whole(), whole()),
        compiler_params=params(),
        name="finish",
    )(gram, sketch)


def solution(mesh):
    placed = (P("space", None), P("space", None), P("probe", None), P())
    return jax.shard_map(
        on_device,
        mesh=mesh,
        in_specs=placed,
        out_specs=(P(None, ("space", "probe")), P()),
        check_vma=False,
    )
```

```python
import functools
import math

import jax
import jax.numpy as jnp
from jax import lax
from jax.experimental import pallas as pl
from jax.experimental.pallas import tpu as pltpu
from jax.sharding import PartitionSpec as P

NZ = 64
SWEEPS = 16
REACH = 2
SPAN = 2 * REACH + 1
GROUP = 16
CHIPS = 8
SLOTS = GROUP * SPAN
QUADS = 8
PAIRS = 32

bound_low = 0.005
bound_high = 24.5

F32 = jnp.float32
VMEM = pltpu.VMEM
SMEM = pltpu.SMEM


def chebyshev_table(count):
    center = 0.5 * (bound_high + bound_low)
    spread = 0.5 * (bound_high - bound_low)
    ratio = center / spread
    rho_prev = 1.0 / ratio
    entries = []
    for index_step in range(count):
        rho_next = 1.0 / (2.0 * ratio - rho_prev)
        entries.append((rho_next * rho_prev, 2.0 * rho_next / spread))
        rho_prev = rho_next
    return entries


def start_scale():
    return 1.0 / (0.5 * (bound_high + bound_low))


def decode(cell):
    cell = jnp.maximum(cell, 0)
    x = lax.shift_right_logical(cell, 13)
    y = lax.bitwise_and(lax.shift_right_logical(cell, 6), 127)
    z = lax.bitwise_and(cell, 63)
    y_first = lax.bitwise_and(y + 1, 126 + 128) - 16
    return x, y, y_first, z, z - 15


def lanes(shape=(8, 128)):
    return lax.broadcasted_iota(jnp.int32, shape, 1)


def sublanes(shape=(8, 128)):
    return lax.broadcasted_iota(jnp.int32, shape, 0)


def wrap(shift):
    return lax.bitwise_and(shift, 127)


OFFSETS = (-2, 2, -1, 1)


def barrier_with(partners):
    barrier = pltpu.get_barrier_semaphore()
    for partner in partners:
        pl.semaphore_signal(barrier, inc=1, device_id=partner, device_id_type=pl.DeviceIdType.MESH)
    return lambda: pl.semaphore_wait(barrier, len(partners))


def remote(src, dst, send, recv, device):
    return pltpu.make_async_remote_copy(
        src_ref=src, dst_ref=dst, send_sem=send, recv_sem=recv, device_id=device, device_id_type=pl.DeviceIdType.MESH
    )


def cut_kernel(cells_ref, cond_ref, leak_ref, out_ref):
    me = lax.axis_index("probe")
    lane = lanes()
    for e in range(SPAN):
        _, _, y_first, _, z_first = decode(cells_ref[me % 2 * (SLOTS // 2) + me // 2 * SPAN + e])
        pair_first = y_first // 2
        shifts = [wrap(128 - z_first), wrap(96 - z_first), wrap(192 - z_first), wrap(160 - z_first)]
        for k in range(QUADS):
            one = pl.multiple_of(jnp.clip(pair_first + 2 * k, 0, 63) * 128, 128)
            two = pl.multiple_of(jnp.clip(pair_first + 2 * k + 1, 0, 63) * 128, 128)
            for prop, ref in enumerate((cond_ref, leak_ref)):
                a = ref[:, pl.ds(one, 128)]
                b = ref[:, pl.ds(two, 128)]
                low = jnp.where(lane < 32, pltpu.roll(a, shifts[0], 1), pltpu.roll(a, shifts[1], 1))
                high = jnp.where(lane < 96, pltpu.roll(b, shifts[2], 1), pltpu.roll(b, shifts[3], 1))
                out_ref[e, prop, k] = jnp.where(lane < 64, low, high)


def faces(cell, here, win_ref, coef):
    _, _, y_first, _, z_first = decode(cell)
    lane = lanes()
    sub = sublanes()
    group = lane // 32
    zz = z_first + lane % 32
    z_ok = (zz >= 0) & (zz < NZ)
    for b in range(SPAN):
        xx = (here + (b - REACH)) * 8 + sub
        x_ok = (xx >= 0) & (xx < 256)
        for k in range(QUADS):
            yy = y_first + 4 * k + group
            inside = x_ok & (yy >= 0) & (yy < 128) & z_ok
            own = win_ref[b, 0, k]
            before = win_ref[max(b - 1, 0), 0, k]
            after = win_ref[min(b + 1, SPAN - 1), 0, k]
            left = win_ref[b, 0, max(k - 1, 0)]
            right = win_ref[b, 0, min(k + 1, QUADS - 1)]
            parts = (
                (jnp.where(sub == 0, pltpu.roll(before, 1, 0), pltpu.roll(own, 1, 0)), xx >= 1),
                (jnp.where(sub == 7, pltpu.roll(after, 7, 0), pltpu.roll(own, 7, 0)), xx < 255),
                (jnp.where(group == 0, pltpu.roll(left, 32, 1), pltpu.roll(own, 32, 1)), yy >= 1),
                (jnp.where(group == 3, pltpu.roll(right, 96, 1), pltpu.roll(own, 96, 1)), yy < 127),
                (pltpu.roll(own, 1, 1), zz >= 1),
                (pltpu.roll(own, 127, 1), zz < NZ - 1),
            )
            diagonal = win_ref[b, 1, k]
            for n, (other, there) in enumerate(parts):
                face = 0.5 * (own + jnp.where(there, other, own))
                diagonal = diagonal + face
                coef[n + 1, b, k] = jnp.where(inside & there, face, 0.0)
            coef[0, b, k] = diagonal


def start_fields(cell, here, search, resid, total):
    x, y, y_first, _, _ = decode(cell)
    lane = lanes()
    sub = sublanes()
    weight = jnp.where(cell >= 0, 1.0, 0.0).astype(F32)
    zero = jnp.zeros((8, 128), F32)
    for b in range(SPAN):
        for k in range(QUADS):
            search[1, b, k] = zero
            if b == REACH and k in (3, 4):
                hit = (sub == x - here * 8) & (4 * k + lane // 32 == y - y_first) & (lane % 32 == 15)
                source = jnp.where(hit, weight, 0.0)
                resid[b, k] = source
                search[0, b, k] = source * start_scale()
            else:
                resid[b, k] = zero
                search[0, b, k] = zero
            total[b, k] = zero


def sweeps(coef, search, resid, total):
    group = lanes() // 32
    sub = sublanes()
    zero = jnp.zeros((8, 128), F32)
    table = chebyshev_table(SWEEPS)
    for j in range(SWEEPS - 1):
        a, c = (float(value) for value in table[j])
        now, later = j % 2, (j + 1) % 2
        wide = j + 1
        k_low, k_high = (15 - wide) // 4, (16 + wide) // 4
        b_low, b_high = (1, 3) if wide <= 8 else (0, 4)
        for b in range(b_low, b_high + 1):
            for k in range(k_low, k_high + 1):
                own = search[now, b, k]
                edge = pltpu.roll(search[now, b - 1, k], 1, 0) if b > 0 else zero
                down = jnp.where(sub == 0, edge, pltpu.roll(own, 1, 0))
                edge = pltpu.roll(search[now, b + 1, k], 7, 0) if b < SPAN - 1 else zero
                up = jnp.where(sub == 7, edge, pltpu.roll(own, 7, 0))
                edge = pltpu.roll(search[now, b, k - 1], 32, 1) if k > 0 else zero
                left = jnp.where(group == 0, edge, pltpu.roll(own, 32, 1))
                edge = pltpu.roll(search[now, b, k + 1], 96, 1) if k < QUADS - 1 else zero
                right = jnp.where(group == 3, edge, pltpu.roll(own, 96, 1))
                image = coef[0, b, k] * own
                image = image - coef[1, b, k] * down
                image = image - coef[2, b, k] * up
                image = image - coef[3, b, k] * left
                image = image - coef[4, b, k] * right
                image = image - coef[5, b, k] * pltpu.roll(own, 1, 1)
                image = image - coef[6, b, k] * pltpu.roll(own, 127, 1)
                rest = resid[b, k] - image
                resid[b, k] = rest
                total[b, k] = total[b, k] + own
                search[later, b, k] = a * own + c * rest


def split2(value):
    high = value.astype(jnp.bfloat16)
    return high, (value - high.astype(F32)).astype(jnp.bfloat16)


def moves(cell):
    shape = (256, 128)
    _, _, y_first, _, z_first = decode(jnp.broadcast_to(cell[0:1, :], shape))
    lane = lanes(shape)
    row = sublanes(shape)
    odd = lax.bitwise_and(lax.shift_right_arithmetic(y_first, 1), 1)
    same_z = lax.bitwise_and(row + z_first, 31) == lax.bitwise_and(lane, 31)
    same_y = lax.bitwise_and(lax.shift_right_logical(row, 5) + 2 * odd, 3) == lax.shift_right_logical(lane, 5)
    hit = same_z & same_y & ((row < 128) == (lane < 64))
    return jnp.where(hit, 1.0, 0.0).astype(jnp.bfloat16)


def align(first, second, b, move, total, out_ref):
    one = split2(jnp.concatenate([total[b, lax.bitwise_and(k - first, 7)] for k in range(QUADS)], axis=0))
    two = split2(jnp.concatenate([total[b, lax.bitwise_and(k - second, 7)] for k in range(QUADS)], axis=0))
    both = jnp.concatenate([jnp.concatenate(part, axis=1) for part in zip(one, two)], axis=0)
    both = jnp.dot(both, move[...], preferred_element_type=F32)
    both = both[:64] + both[64:]
    for k in range(QUADS):
        out_ref[b, :, k, :] = both[8 * k : 8 * k + 8]


def panel(signs, slot_ref, cell_lane, cell_down, half, keep, before_ref, rows_ref, out_ref):
    table = jnp.concatenate([signs[p % 2, p // 2] for p in range(GROUP)], axis=0)
    table = (2 * table - 1).astype(jnp.bfloat16)
    which = lax.broadcasted_iota(jnp.int32, (256, 128), 0) == slot_ref[...]
    pick = jnp.dot(table, which.astype(F32).astype(jnp.bfloat16), preferred_element_type=F32)
    _, _, y_first, _, _ = decode(cell_lane[...])
    pair_first = lax.shift_right_arithmetic(y_first, 1) - PAIRS * half
    _, _, _, _, z_first = decode(cell_down[...])
    lane = lanes((SLOTS, 128))
    z_here = lane % 64 - z_first
    shown = (z_here >= 0) & (z_here < 32)
    group = lane // 32
    blank = jnp.zeros((128 - SLOTS, 128), jnp.bfloat16)
    for k in range(QUADS):
        own = rows_ref[pl.ds(k, SLOTS, stride=8), :]
        r1, r2, r3 = (pltpu.roll(own, 32 * n, 1) for n in (1, 2, 3))
        pairs = (
            jnp.where(group == 0, own, jnp.where(group == 3, r2, r1)),
            jnp.where(group == 0, r2, jnp.where(group == 3, own, r3)),
        )
        for m in range(2):
            high, low = split2(jnp.where(shown, pairs[m], 0.0))
            value = jnp.concatenate([high, blank, low, blank], axis=0)
            left = []
            for t in (2 * k + m, 2 * k + m + 16):
                ok = (pair_first <= t) & (t < pair_first + 16)
                left.append(jnp.where(ok, pick, 0.0).astype(jnp.bfloat16))
            left = jnp.concatenate(left, axis=0)
            both = jnp.dot(jnp.concatenate([left, left], axis=1), value, preferred_element_type=F32)
            for n in range(2):
                at = 128 * (2 * k + m + 16 * n)
                part = both[64 * n : 64 * n + 64]
                out_ref[:, at : at + 128] = part + keep * before_ref[:, at : at + 128]


def gram_of(sketch_ref):
    both = jnp.concatenate(split2(sketch_ref[...]), axis=0)
    full = lax.dot_general(both, both, (((1,), (1,)), ((), ())), preferred_element_type=F32)
    return full[:64, :64] + ((full[:64, 64:] + full[64:, :64]) + full[64:, 64:])


def sketch_kernel(
    own_scalar,
    own_cell,
    keep_ref,
    cuts,
    signs_ref,
    slot_ref,
    cell_lane,
    cell_down,
    before_ref,
    sketch_ref,
    gram_ref,
    win,
    signs,
    coef,
    search,
    resid,
    total,
    fields,
    block,
    rows,
    move,
    mine,
    twin_buf,
    y_buf,
    z_buf,
    x_buf,
    win_sem,
    sign_sem,
    sign_pair,
    near_sem,
    row_sem,
    pair_sem,
    twin_sem,
    y_sem,
    z_sem,
    x_sem,
    last_sem,
):
    count = lax.axis_size("space")
    here = lax.axis_index("space")
    me = lax.axis_index("probe")
    chip = me // 2
    core = me % 2
    x = here // 8
    z = here % 8
    near = [(lax.rem(here + d + count, count), me) for d in OFFSETS]
    along = [(here, lax.rem(chip + r, CHIPS) * 2 + core) for r in range(1, CHIPS)]
    ring_z = [(x * 8 + lax.rem(z + r, 8), me) for r in range(1, 8)]
    ring_x = [(lax.rem(x + r, 4) * 8 + z, me) for r in range(1, 4)]
    twin = (here, chip * 2 + 1 - core)
    entered = barrier_with(near + along + [twin] + ring_z + ring_x)
    cell = own_cell[...]
    start_fields(cell, here, search, resid, total)
    move[...] = moves(cell)
    entered()
    sent = []
    windows = []
    for i, d in enumerate(OFFSETS):
        copy = remote(cuts.at[d + 2], win.at[2 - d], win_sem.at[0, i], win_sem.at[1, i], near[i])
        copy.start()
        windows.append(copy)
    shared = []
    for r in range(1, CHIPS):
        copy = remote(signs_ref, signs.at[core, chip], sign_sem.at[0, r], sign_sem.at[1, r], along[r - 1])
        copy.start()
        shared.append(copy)
    win[REACH] = cuts[REACH]
    signs[core, chip] = signs_ref[...]
    for copy in windows:
        copy.wait_recv()
    faces(cell, here, win, coef)
    sweeps(coef, search, resid, total)
    spread = []
    last = (SWEEPS - 1) % 2
    for b in range(SPAN):
        for k in range(QUADS):
            total[b, k] = total[b, k] + search[last, b, k]
    _, _, y_first, _, _ = decode(own_scalar[0])
    second = lax.shift_right_arithmetic(y_first, 2)
    first = second + lax.bitwise_and(lax.shift_right_arithmetic(y_first, 1), 1)
    for i, d in enumerate(OFFSETS):
        align(first, second, d + 2, move, total, fields)
        copy = remote(
            fields.at[d + 2], block.at[:, pl.ds(8 * (2 - d), 8)], near_sem.at[0, i], near_sem.at[1, i], near[i]
        )
        copy.start()
        spread.append(copy)
    align(first, second, REACH, move, total, fields)
    block[:, 8 * REACH : 8 * REACH + 8] = fields[REACH]
    for copy in shared:
        copy.wait_recv()
    pair = remote(signs.at[core], signs.at[core], sign_pair.at[0], sign_pair.at[1], twin)
    pair.start()
    sent += windows + shared + spread + [pair]
    for copy in spread:
        copy.wait_recv()
    out = []
    place = pl.ds(pl.multiple_of((core * CHIPS + chip) * 8 * SPAN, 8), 8 * SPAN)
    for r in range(1, CHIPS):
        target = lax.rem(chip + r, CHIPS)
        copy = remote(block.at[target], rows.at[place], row_sem.at[0, r], row_sem.at[1, r], along[r - 1])
        copy.start()
        out.append(copy)
    rows[place, :] = block[chip]
    pairs = []
    for r in (0, 1, 7, 2, 6, 3, 5, 4):
        source = lax.rem(chip - r + CHIPS, CHIPS)
        if r:
            out[r - 1].wait_recv()
        part = rows.at[pl.ds(pl.multiple_of((core * CHIPS + source) * 8 * SPAN, 8), 8 * SPAN)]
        copy = remote(part, part, pair_sem.at[0, r], pair_sem.at[1, r], twin)
        copy.start()
        pairs.append(copy)
    pair.wait_recv()
    for copy in pairs:
        copy.wait_recv()
    sent += out + pairs
    panel(signs, slot_ref, cell_lane, cell_down, core, keep_ref[...], before_ref, rows, sketch_ref)
    gram = gram_of(sketch_ref)
    for h in range(2):
        mine[h] = jnp.concatenate([gram[32 * h : 32 * h + 16], gram[32 * h + 16 : 32 * h + 32]], axis=1)
    copy = remote(mine.at[1 - core], twin_buf, twin_sem.at[0], twin_sem.at[1], twin)
    copy.start()
    sent.append(copy)
    copy.wait_recv()
    value = mine[core] + twin_buf[...]
    for buf, sem, at, ring in ((y_buf, y_sem, chip, along), (z_buf, z_sem, z, ring_z), (x_buf, x_sem, x, ring_x)):
        buf[at] = value
        steps = []
        for r, device in enumerate(ring):
            copy = remote(buf.at[at], buf.at[at], sem.at[0, r], sem.at[1, r], device)
            copy.start()
            steps.append(copy)
        for copy in steps:
            copy.wait_recv()
        sent += steps
        value = buf[0]
        for r in range(1, len(ring) + 1):
            value = value + buf[r]
    gram_ref[core] = value
    copy = remote(gram_ref.at[core], gram_ref.at[core], last_sem.at[0], last_sem.at[1], twin)
    copy.start()
    copy.wait_recv()
    for item in sent + [copy]:
        item.wait_send()


def finish_kernel(gram_ref, sketch_ref, basis_ref, factor_ref):
    shape = (8, 128)
    lane = lanes(shape)
    sub = sublanes(shape)
    rows = []
    for i in range(8):
        block = gram_ref[i // 4, 8 * (i % 2) : 8 * (i % 2) + 8, :]
        if i % 4 >= 2:
            block = pltpu.roll(block, 64, 1)
        rows.append(jnp.where(lane < 64, block, jnp.where(lane - 64 == sub + 8 * i, 1.0, 0.0)))
    for n in range(8):
        columns = [[jnp.broadcast_to(rows[i][:, 8 * n + c : 8 * n + c + 1], shape) for i in range(n, 8)] for c in range(8)]
        own = rows[n]
        lines = []
        for c in range(8):
            pivot = jnp.broadcast_to(columns[c][0][c : c + 1, :], shape)
            scale = lax.rsqrt(pivot)
            scale = scale * (1.5 - 0.5 * pivot * scale * scale)
            line = jnp.broadcast_to(own[c : c + 1, :], shape) * scale
            columns[c] = [value * scale for value in columns[c]]
            below = jnp.where(sub > c, columns[c][0], 0.0)
            own = jnp.where(sub == c, line, own - below * line)
            for later in range(c + 1, 8):
                factor = jnp.broadcast_to(columns[c][0][later : later + 1, :], shape)
                columns[later][0] = columns[later][0] - below * factor
                for i in range(1, 8 - n):
                    columns[later][i] = columns[later][i] - columns[c][i] * factor
            lines.append(line)
        rows[n] = own
        for i in range(n + 1, 8):
            value = rows[i]
            for c in range(8):
                value = value - columns[c][i - n] * lines[c]
            rows[i] = value
    full = jnp.concatenate(rows, axis=0)
    row_at = lax.broadcasted_iota(jnp.int32, (64, 64), 0)
    col_at = lax.broadcasted_iota(jnp.int32, (64, 64), 1)
    upper = jnp.where(col_at >= row_at, full[:, :64], 0.0)
    factor_ref[...] = upper * (1.0 / math.sqrt(256))
    high, low = split2(full[:, 64:] * math.sqrt(256 * 128 * 64))
    left = jnp.concatenate([high, high, low], axis=1)
    for t in range(8):
        high, low = split2(sketch_ref[:, 512 * t : 512 * t + 512])
        right = jnp.concatenate([high, low, high], axis=0)
        basis_ref[:, 512 * t : 512 * t + 512] = jnp.dot(left, right, preferred_element_type=F32)


def params(**more):
    return pltpu.CompilerParams(vmem_limit_bytes=48 * 1024 * 1024, **more)


def whole(space=VMEM):
    return pl.BlockSpec(memory_space=space)


def dma(*shape):
    return pltpu.SemaphoreType.DMA(shape)


def on_device(conductivity, leakage, signs, wells):
    here = lax.axis_index("space")
    chip = lax.axis_index("probe") // 2
    core = lax.axis_index("probe") % 2
    cells = conductivity.shape[0] * conductivity.shape[1]
    probes = signs.shape[0] * GROUP
    count = wells.shape[0]
    owner = wells // cells
    index = jnp.arange(count, dtype=jnp.int32)
    rank = jnp.sum((owner[None, :] == owner[:, None]) & (index[None, :] < index[:, None]), axis=1, dtype=jnp.int32)
    rounds = jnp.max(rank) // GROUP + 1
    slot = jnp.arange(128, dtype=jnp.int32)
    slot_probe = jnp.where(slot < SLOTS, (slot % (SLOTS // 2)) // SPAN * 2 + slot // (SLOTS // 2), count)
    slot_block = here + slot % SPAN - REACH

    def body(carry):
        turn, sketch, _ = carry
        match = (owner[None, :] == slot_block[:, None]) & (rank[None, :] - turn * GROUP == slot_probe[:, None])
        chosen = jnp.max(jnp.where(match, index[None, :], -1), axis=1)
        cell = jnp.max(jnp.where(match, wells[None, :], -1), axis=1)
        cuts = pl.pallas_call(
            cut_kernel,
            out_shape=jax.ShapeDtypeStruct((SPAN, 2, QUADS, 8, 128), F32),
            in_specs=[whole(SMEM), whole(), whole()],
            out_specs=whole(),
            compiler_params=params(),
            name="cut",
        )(cell, conductivity, leakage)
        own = cell[core * (SLOTS // 2) + chip * SPAN + REACH]
        field = VMEM((SPAN, QUADS, 8, 128), F32)
        sketch, gram = pl.pallas_call(
            sketch_kernel,
            out_shape=(
                jax.ShapeDtypeStruct(sketch.shape, F32),
                jax.ShapeDtypeStruct((2, 16, 128), F32),
            ),
            in_specs=[whole(SMEM)] + [whole()] * 8,
            out_specs=(whole(), whole()),
            scratch_shapes=[
                VMEM((SPAN, 2, QUADS, 8, 128), F32),
                VMEM((2, CHIPS, probes // GROUP, count), jnp.int32),
                VMEM((7, SPAN, QUADS, 8, 128), F32),
                VMEM((2, SPAN, QUADS, 8, 128), F32),
                field,
                field,
                VMEM((SPAN, 8, QUADS, 128), F32),
                VMEM((8, SPAN * QUADS, 128), F32),
                VMEM((SLOTS * QUADS, 128), F32),
                VMEM((256, 128), jnp.bfloat16),
                VMEM((2, 16, 128), F32),
                VMEM((16, 128), F32),
                VMEM((8, 16, 128), F32),
                VMEM((8, 16, 128), F32),
                VMEM((4, 16, 128), F32),
                dma(2, 4),
                dma(2, 8),
                dma(2),
                dma(2, 4),
                dma(2, 8),
                dma(2, 8),
                dma(2),
                dma(2, 8),
                dma(2, 8),
                dma(2, 4),
                dma(2),
            ],
            compiler_params=params(collective_id=0, has_side_effects=True),
            name="sketch",
        )(
            own.reshape(1),
            jnp.broadcast_to(own, (8, 128)),
            jnp.broadcast_to((turn > 0).astype(F32), (1, 128)),
            cuts,
            signs,
            chosen[None, :],
            cell[None, :],
            jnp.broadcast_to(cell[:SLOTS, None], (SLOTS, 128)),
            sketch,
        )
        return turn + 1, sketch, gram

    sketch = jnp.zeros((probes, cells // GROUP), F32)
    gram = jnp.zeros((2, 16, 128), F32)
    _, sketch, gram = lax.while_loop(lambda carry: carry[0] < rounds, body, (jnp.int32(0), sketch, gram))
    return pl.pallas_call(
        finish_kernel,
        out_shape=(
            jax.ShapeDtypeStruct((probes, cells // GROUP), F32),
            jax.ShapeDtypeStruct((probes, probes), F32),
        ),
        in_specs=[whole(), whole()],
        out_specs=(whole(), whole()),
        compiler_params=params(),
        name="finish",
    )(gram, sketch)


def solution(mesh):
    placed = (P("space", None), P("space", None), P("probe", None), P())
    return jax.shard_map(
        on_device,
        mesh=mesh,
        in_specs=placed,
        out_specs=(P(None, ("space", "probe")), P()),
        check_vma=False,
    )
```

```python
import functools
import math

import jax
import jax.numpy as jnp
from jax import lax
from jax.experimental import pallas as pl
from jax.experimental.pallas import tpu as pltpu
from jax.sharding import PartitionSpec as P

NZ = 64
SWEEPS = 16
REACH = 2
SPAN = 2 * REACH + 1
GROUP = 16
CHIPS = 8
SLOTS = GROUP * SPAN
QUADS = 8
PAIRS = 32

bound_low = 0.005
bound_high = 24.5

F32 = jnp.float32
VMEM = pltpu.VMEM
SMEM = pltpu.SMEM


def chebyshev_table(count):
    center = 0.5 * (bound_high + bound_low)
    spread = 0.5 * (bound_high - bound_low)
    ratio = center / spread
    rho_prev = 1.0 / ratio
    entries = []
    for index_step in range(count):
        rho_next = 1.0 / (2.0 * ratio - rho_prev)
        entries.append((rho_next * rho_prev, 2.0 * rho_next / spread))
        rho_prev = rho_next
    return entries


def start_scale():
    return 1.0 / (0.5 * (bound_high + bound_low))


def decode(cell):
    cell = jnp.maximum(cell, 0)
    x = lax.shift_right_logical(cell, 13)
    y = lax.bitwise_and(lax.shift_right_logical(cell, 6), 127)
    z = lax.bitwise_and(cell, 63)
    y_first = lax.bitwise_and(y + 1, 126 + 128) - 16
    return x, y, y_first, z, z - 15


def lanes(shape=(8, 128)):
    return lax.broadcasted_iota(jnp.int32, shape, 1)


def sublanes(shape=(8, 128)):
    return lax.broadcasted_iota(jnp.int32, shape, 0)


def wrap(shift):
    return lax.bitwise_and(shift, 127)


OFFSETS = (-2, 2, -1, 1)


def barrier_with(partners):
    barrier = pltpu.get_barrier_semaphore()
    for partner in partners:
        pl.semaphore_signal(barrier, inc=1, device_id=partner, device_id_type=pl.DeviceIdType.MESH)
    return lambda: pl.semaphore_wait(barrier, len(partners))


def remote(src, dst, send, recv, device):
    return pltpu.make_async_remote_copy(
        src_ref=src, dst_ref=dst, send_sem=send, recv_sem=recv, device_id=device, device_id_type=pl.DeviceIdType.MESH
    )


def quads(block):
    return range(QUADS) if 0 < block < SPAN - 1 else range(2, 6)


def counted(owner, first, rows):
    shape = (rows, 256)
    lane = lanes(shape)
    ones = jnp.where(jnp.broadcast_to(owner, shape) == sublanes(shape) + first, 1, 0)
    total = ones
    for step in (1, 2, 4, 8, 16, 32, 64, 128):
        total = total + jnp.where(lane >= step, pltpu.roll(total, step, 1), 0)
    return ones, total - ones


def cut(cell, cell_row, e, cond_ref, leak_ref, out_ref):
    pair_first = lax.shift_right_arithmetic(decode(cell)[2], 1)
    shape = (256, 128)
    z_first = decode(jnp.broadcast_to(cell_row, shape))[4]
    row = sublanes(shape)
    lane = lanes(shape)
    same = lax.shift_right_logical(row, 6) == lax.shift_right_logical(lane, 5)
    hit = same & (lax.bitwise_and(row, 63) - z_first == lax.bitwise_and(lane, 31))
    move = jnp.where(hit, 1.0, 0.0).astype(jnp.bfloat16)
    parts = []
    for ref in (cond_ref, leak_ref):
        for k in quads(e):
            one = ref[jnp.clip(pair_first + 2 * k, 0, 63)]
            two = ref[jnp.clip(pair_first + 2 * k + 1, 0, 63)]
            parts.append(jnp.concatenate([one, two], axis=1))
    rows = 8 * len(parts)
    both = jnp.concatenate(split2(jnp.concatenate(parts, axis=0)), axis=0)
    both = jnp.dot(both, move, preferred_element_type=F32)
    both = both[:rows] + both[rows:]
    for n, k in enumerate(quads(e)):
        for prop in range(2):
            at = 8 * (n + prop * len(quads(e)))
            out_ref[e, prop, k] = both[at : at + 8]


def faces(cell, here, win_ref, coef):
    _, _, y_first, _, z_first = decode(cell)
    lane = lanes()
    sub = sublanes()
    group = lane // 32
    zz = z_first + lane % 32
    z_ok = (zz >= 0) & (zz < NZ)
    for b in range(SPAN):
        xx = (here + (b - REACH)) * 8 + sub
        x_ok = (xx >= 0) & (xx < 256)
        for k in quads(b):
            yy = y_first + 4 * k + group
            inside = x_ok & (yy >= 0) & (yy < 128) & z_ok
            own = win_ref[b, 0, k]
            before = win_ref[max(b - 1, 0), 0, k]
            after = win_ref[min(b + 1, SPAN - 1), 0, k]
            left = win_ref[b, 0, max(k - 1, 0)]
            right = win_ref[b, 0, min(k + 1, QUADS - 1)]
            parts = (
                (jnp.where(sub == 0, pltpu.roll(before, 1, 0), pltpu.roll(own, 1, 0)), xx >= 1),
                (jnp.where(sub == 7, pltpu.roll(after, 7, 0), pltpu.roll(own, 7, 0)), xx < 255),
                (jnp.where(group == 0, pltpu.roll(left, 32, 1), pltpu.roll(own, 32, 1)), yy >= 1),
                (jnp.where(group == 3, pltpu.roll(right, 96, 1), pltpu.roll(own, 96, 1)), yy < 127),
                (pltpu.roll(own, 1, 1), zz >= 1),
                (pltpu.roll(own, 127, 1), zz < NZ - 1),
            )
            diagonal = win_ref[b, 1, k]
            for n, (other, there) in enumerate(parts):
                face = 0.5 * (own + jnp.where(there, other, own))
                diagonal = diagonal + face
                coef[n + 1, b, k] = jnp.where(inside & there, face, 0.0)
            coef[0, b, k] = diagonal


def start_fields(cell, here, search, resid, total):
    x, y, y_first, _, _ = decode(cell)
    lane = lanes()
    sub = sublanes()
    weight = jnp.where(cell >= 0, 1.0, 0.0).astype(F32)
    zero = jnp.zeros((8, 128), F32)
    for b in range(SPAN):
        for k in range(QUADS):
            search[1, b, k] = zero
            if b == REACH and k in (3, 4):
                hit = (sub == x - here * 8) & (4 * k + lane // 32 == y - y_first) & (lane % 32 == 15)
                source = jnp.where(hit, weight, 0.0)
                resid[b, k] = source
                search[0, b, k] = source * start_scale()
            else:
                resid[b, k] = zero
                search[0, b, k] = zero
            total[b, k] = zero


def sweeps(coef, search, resid, total):
    group = lanes() // 32
    sub = sublanes()
    zero = jnp.zeros((8, 128), F32)
    table = chebyshev_table(SWEEPS)
    for j in range(SWEEPS - 1):
        a, c = (float(value) for value in table[j])
        now, later = j % 2, (j + 1) % 2
        wide = j + 1
        k_low, k_high = (15 - wide) // 4, (16 + wide) // 4
        b_low, b_high = (1, 3) if wide <= 8 else (0, 4)
        for b in range(b_low, b_high + 1):
            for k in range(max(k_low, quads(b)[0]), min(k_high, quads(b)[-1]) + 1):
                own = search[now, b, k]
                edge = pltpu.roll(search[now, b - 1, k], 1, 0) if b > 0 else zero
                down = jnp.where(sub == 0, edge, pltpu.roll(own, 1, 0))
                edge = pltpu.roll(search[now, b + 1, k], 7, 0) if b < SPAN - 1 else zero
                up = jnp.where(sub == 7, edge, pltpu.roll(own, 7, 0))
                edge = pltpu.roll(search[now, b, k - 1], 32, 1) if k > 0 else zero
                left = jnp.where(group == 0, edge, pltpu.roll(own, 32, 1))
                edge = pltpu.roll(search[now, b, k + 1], 96, 1) if k < QUADS - 1 else zero
                right = jnp.where(group == 3, edge, pltpu.roll(own, 96, 1))
                image = coef[0, b, k] * own
                image = image - coef[1, b, k] * down
                image = image - coef[2, b, k] * up
                image = image - coef[3, b, k] * left
                image = image - coef[4, b, k] * right
                image = image - coef[5, b, k] * pltpu.roll(own, 1, 1)
                image = image - coef[6, b, k] * pltpu.roll(own, 127, 1)
                rest = resid[b, k] - image
                resid[b, k] = rest
                total[b, k] = total[b, k] + own
                search[later, b, k] = a * own + c * rest


def split2(value):
    high = value.astype(jnp.bfloat16)
    return high, (value - high.astype(F32)).astype(jnp.bfloat16)


def moves(cell):
    shape = (256, 128)
    _, _, y_first, _, z_first = decode(jnp.broadcast_to(cell[0:1, :], shape))
    lane = lanes(shape)
    row = sublanes(shape)
    odd = lax.bitwise_and(lax.shift_right_arithmetic(y_first, 1), 1)
    same_z = lax.bitwise_and(row + z_first, 31) == lax.bitwise_and(lane, 31)
    same_y = lax.bitwise_and(lax.shift_right_logical(row, 5) + 2 * odd, 3) == lax.shift_right_logical(lane, 5)
    hit = same_z & same_y & ((row < 128) == (lane < 64))
    return jnp.where(hit, 1.0, 0.0).astype(jnp.bfloat16)


def align(first, second, b, move, total, out_ref):
    one = split2(jnp.concatenate([total[b, lax.bitwise_and(k - first, 7)] for k in range(QUADS)], axis=0))
    two = split2(jnp.concatenate([total[b, lax.bitwise_and(k - second, 7)] for k in range(QUADS)], axis=0))
    both = jnp.concatenate([jnp.concatenate(part, axis=1) for part in zip(one, two)], axis=0)
    both = jnp.dot(both, move[...], preferred_element_type=F32)
    both = both[:64] + both[64:]
    for k in range(QUADS):
        out_ref[b, :, k, :] = both[8 * k : 8 * k + 8]


def slots(ones, counts, wells, turn, chip):
    shape = (GROUP, 256)
    place = sublanes(shape)
    probe = 2 * lax.bitwise_and(chip - lax.bitwise_and(place, 7), 7) + lax.shift_right_logical(place, 3)
    want = probe + GROUP * jnp.broadcast_to(turn, shape)
    parts = []
    for e in range(SPAN):
        there = jnp.broadcast_to(ones[e : e + 1], shape) > 0
        parts.append(there & (jnp.broadcast_to(counts[e : e + 1], shape) == want))
    holds = [jnp.where(part, 1.0, 0.0) for part in parts]
    wells = jnp.broadcast_to(wells, shape)
    cells = [jnp.max(jnp.where(part, wells, -1), axis=1, keepdims=True) for part in parts]
    return jnp.concatenate(holds, axis=0), jnp.concatenate(cells, axis=0)


def panel(pick, pair_first, z_first, half, keep, before_ref, rows_ref, out_ref):
    pair_first = pair_first - float(PAIRS) * half.astype(F32)
    lane = lanes((SLOTS, 128))
    z_here = lane % 64 - z_first
    shown = (z_here >= 0) & (z_here < 32)
    group = lane // 32
    blank = jnp.zeros((128 - SLOTS, 128), jnp.bfloat16)
    for k in range(QUADS):
        own = rows_ref[pl.ds(k, SLOTS, stride=8), :]
        r1, r2, r3 = (pltpu.roll(own, 32 * n, 1) for n in (1, 2, 3))
        pairs = (
            jnp.where(group == 0, own, jnp.where(group == 3, r2, r1)),
            jnp.where(group == 0, r2, jnp.where(group == 3, own, r3)),
        )
        for m in range(2):
            high, low = split2(jnp.where(shown, pairs[m], 0.0))
            value = jnp.concatenate([high, blank, low, blank], axis=0)
            left = []
            for t in (2 * k + m, 2 * k + m + 16):
                ok = (pair_first <= t) & (t < pair_first + 16)
                left.append(jnp.where(ok, pick, 0.0).astype(jnp.bfloat16))
            left = jnp.concatenate(left, axis=0)
            both = jnp.dot(jnp.concatenate([left, left], axis=1), value, preferred_element_type=F32)
            for n in range(2):
                at = 128 * (2 * k + m + 16 * n)
                part = both[64 * n : 64 * n + 64]
                out_ref[:, at : at + 128] = part + keep * before_ref[:, at : at + 128]


def gram_of(sketch_ref):
    both = jnp.concatenate(split2(sketch_ref[...]), axis=0)
    full = lax.dot_general(both, both, (((1,), (1,)), ((), ())), preferred_element_type=F32)
    return full[:64, :64] + ((full[:64, 64:] + full[64:, :64]) + full[64:, 64:])


def sketch_kernel(
    turn_ref,
    wells_hbm,
    cond_hbm,
    leak_hbm,
    signs_hbm,
    before_ref,
    sketch_ref,
    gram_ref,
    rounds_ref,
    wells_ref,
    cond_ref,
    leak_ref,
    cond_pairs,
    leak_pairs,
    cuts,
    win,
    signs,
    coef,
    search,
    resid,
    total,
    fields,
    rows,
    move,
    pick_ref,
    first_ref,
    depth_ref,
    mine,
    twin_buf,
    y_buf,
    z_buf,
    x_buf,
    load_sem,
    win_sem,
    sign_sem,
    sign_pair,
    row_send,
    row_recv,
    pair_sem,
    twin_sem,
    y_sem,
    z_sem,
    x_sem,
    last_sem,
):
    count = lax.axis_size("space")
    here = lax.axis_index("space")
    me = lax.axis_index("probe")
    chip = me // 2
    core = me % 2
    x = here // 8
    z = here % 8
    near = [(lax.rem(here + d + count, count), me) for d in OFFSETS]
    along = [(here, lax.rem(chip + r, CHIPS) * 2 + core) for r in range(1, CHIPS)]
    ring_z = [(x * 8 + lax.rem(z + r, 8), me) for r in range(1, 8)]
    ring_x = [(lax.rem(x + r, 4) * 8 + z, me) for r in range(1, 4)]
    twin = (here, chip * 2 + 1 - core)
    entered = barrier_with(near + along + [twin] + ring_z + ring_x)
    loads = []
    pieces = ((wells_hbm, wells_ref), (cond_hbm, cond_ref), (leak_hbm, leak_ref), (signs_hbm, signs.at[core, chip]))
    for i, (src, dst) in enumerate(pieces):
        loads.append(pltpu.make_async_copy(src, dst, load_sem.at[i]))
        loads[-1].start()
    one = jnp.ones((8, 128), F32)
    for b in (0, SPAN - 1):
        for k in range(QUADS):
            if k not in quads(b):
                win[b, 0, k] = one
    loads[0].wait()
    wells = wells_ref[...]
    turn = turn_ref[...]
    owner = lax.shift_right_logical(wells, 16)
    ones, counts = counted(owner, here - REACH, 8)
    chosen = (ones > 0) & (counts == me + GROUP * jnp.broadcast_to(turn, (8, 256)))
    cells = jnp.max(jnp.where(chosen, jnp.broadcast_to(wells, (8, 256)), -1), axis=1, keepdims=True)
    cell = jnp.broadcast_to(cells[REACH : REACH + 1], (8, 128))
    for copy in loads[1:]:
        copy.wait()
    for src, dst in ((cond_ref, cond_pairs), (leak_ref, leak_pairs)):
        for t in range(64):
            dst[t] = src[:, 128 * t : 128 * t + 128]
    for e in range(SPAN):
        cut(cells[e, 0], cells[e : e + 1], e, cond_pairs, leak_pairs, cuts)
    entered()
    sent = []
    windows = []
    for i, d in enumerate(OFFSETS):
        src, dst = cuts.at[d + 2], win.at[2 - d]
        if d in (-2, 2):
            src, dst = cuts.at[d + 2, :, pl.ds(2, 4)], win.at[2 - d, :, pl.ds(2, 4)]
        copy = remote(src, dst, win_sem.at[0, i], win_sem.at[1, i], near[i])
        copy.start()
        windows.append(copy)
    shared = []
    for r in range(1, CHIPS):
        part = signs.at[core, chip]
        copy = remote(part, part, sign_sem.at[0, r], sign_sem.at[1, r], along[r - 1])
        copy.start()
        shared.append(copy)
    win[REACH] = cuts[REACH]
    start_fields(cell, here, search, resid, total)
    move[...] = moves(cell)
    all_ones, all_counts = counted(owner, 0, count)
    rounds_ref[0] = lax.shift_right_logical(jnp.max(jnp.where(all_ones > 0, all_counts, 0)), 4) + 1
    holds, slot_cells = slots(ones, counts, wells, turn, chip)
    _, _, y_first, _, z_first = decode(jnp.broadcast_to(slot_cells, (SLOTS, 128)))
    depth_ref[...] = z_first
    pairs_first = lax.shift_right_arithmetic(y_first, 1).astype(F32)
    pairs_first = jnp.concatenate([pairs_first, jnp.zeros((128 - SLOTS, 128), F32)], axis=0)
    first_ref[...] = pairs_first.T
    for copy in windows:
        copy.wait_recv()
    faces(cell, here, win, coef)
    sweeps(coef, search, resid, total)
    last = (SWEEPS - 1) % 2
    for b in range(SPAN):
        for k in range(QUADS):
            total[b, k] = total[b, k] + search[last, b, k]
    y_first = decode(cells[REACH, 0])[2]
    second = lax.shift_right_arithmetic(y_first, 2)
    first = second + lax.bitwise_and(lax.shift_right_arithmetic(y_first, 1), 1)
    arrivals = {}
    for d in OFFSETS + (0,):
        align(first, second, d + 2, move, total, fields)
        e = 2 - d
        for r in (4, 3, 5, 2, 6, 1, 7, 0):
            target = lax.rem(chip + r, CHIPS)
            place = rows.at[pl.ds(pl.multiple_of((e * GROUP + core * CHIPS + r) * 8, 8), 8)]
            if d == 0 and r == 0:
                rows[pl.ds(pl.multiple_of((e * GROUP + core * CHIPS) * 8, 8), 8), :] = fields[REACH, chip]
                continue
            device = (lax.rem(here + d + count, count), target * 2 + core)
            copy = remote(fields.at[d + 2, target], place, row_send.at[d + 2, r], row_recv.at[e, r], device)
            copy.start()
            arrivals[e, r] = copy
    for copy in shared:
        copy.wait_recv()
    pair = remote(signs.at[core], signs.at[core], sign_pair.at[0], sign_pair.at[1], twin)
    pair.start()
    pair.wait_recv()
    table = jnp.concatenate([signs[p % 2, p // 2] for p in range(GROUP)], axis=0)
    table = (2 * table - 1).astype(F32).astype(jnp.bfloat16)
    holds = jnp.concatenate([holds, jnp.zeros((128 - SLOTS, 256), F32)], axis=0).astype(jnp.bfloat16)
    pick_ref[...] = lax.dot_general(table, holds, (((1,), (1,)), ((), ())), preferred_element_type=F32)
    pairs = []
    for e in (2, 1, 3, 0, 4):
        for r in range(CHIPS):
            if (e, r) != (REACH, 0):
                arrivals[e, r].wait_recv()
        part = rows.at[pl.ds(pl.multiple_of((e * GROUP + core * CHIPS) * 8, 8), 8 * CHIPS)]
        copy = remote(part, part, pair_sem.at[0, e], pair_sem.at[1, e], twin)
        copy.start()
        pairs.append(copy)
    for copy in pairs:
        copy.wait_recv()
    sent += windows + shared + [pair] + list(arrivals.values()) + pairs
    keep = jnp.where(turn[:, :128] > 0, 1.0, 0.0)
    panel(pick_ref[...], first_ref[0:1, :], depth_ref[...], core, keep, before_ref, rows, sketch_ref)
    gram = gram_of(sketch_ref)
    for h in range(2):
        mine[h] = jnp.concatenate([gram[32 * h : 32 * h + 16], gram[32 * h + 16 : 32 * h + 32]], axis=1)
    copy = remote(mine.at[1 - core], twin_buf, twin_sem.at[0], twin_sem.at[1], twin)
    copy.start()
    sent.append(copy)
    copy.wait_recv()
    value = mine[core] + twin_buf[...]
    for buf, sem, at, ring in ((y_buf, y_sem, chip, along), (z_buf, z_sem, z, ring_z), (x_buf, x_sem, x, ring_x)):
        buf[at] = value
        steps = []
        for r, device in enumerate(ring):
            copy = remote(buf.at[at], buf.at[at], sem.at[0, r], sem.at[1, r], device)
            copy.start()
            steps.append(copy)
        for copy in steps:
            copy.wait_recv()
        sent += steps
        value = buf[0]
        for r in range(1, len(ring) + 1):
            value = value + buf[r]
    gram_ref[core] = value
    copy = remote(gram_ref.at[core], gram_ref.at[core], last_sem.at[0], last_sem.at[1], twin)
    copy.start()
    copy.wait_recv()
    for item in sent + [copy]:
        item.wait_send()


def finish_kernel(gram_ref, sketch_ref, basis_ref, factor_ref):
    shape = (8, 128)
    lane = lanes(shape)
    sub = sublanes(shape)
    rows = []
    for i in range(8):
        block = gram_ref[i // 4, 8 * (i % 2) : 8 * (i % 2) + 8, :]
        if i % 4 >= 2:
            block = pltpu.roll(block, 64, 1)
        rows.append(jnp.where(lane < 64, block, jnp.where(lane - 64 == sub + 8 * i, 1.0, 0.0)))
    for n in range(8):
        columns = [[jnp.broadcast_to(rows[i][:, 8 * n + c : 8 * n + c + 1], shape) for i in range(n, 8)] for c in range(8)]
        own = rows[n]
        lines = []
        for c in range(8):
            pivot = jnp.broadcast_to(columns[c][0][c : c + 1, :], shape)
            scale = lax.rsqrt(pivot)
            scale = scale * (1.5 - 0.5 * pivot * scale * scale)
            line = jnp.broadcast_to(own[c : c + 1, :], shape) * scale
            columns[c] = [value * scale for value in columns[c]]
            below = jnp.where(sub > c, columns[c][0], 0.0)
            own = jnp.where(sub == c, line, own - below * line)
            for later in range(c + 1, 8):
                factor = jnp.broadcast_to(columns[c][0][later : later + 1, :], shape)
                columns[later][0] = columns[later][0] - below * factor
                for i in range(1, 8 - n):
                    columns[later][i] = columns[later][i] - columns[c][i] * factor
            lines.append(line)
        rows[n] = own
        for i in range(n + 1, 8):
            value = rows[i]
            for c in range(8):
                value = value - columns[c][i - n] * lines[c]
            rows[i] = value
    full = jnp.concatenate(rows, axis=0)
    row_at = lax.broadcasted_iota(jnp.int32, (64, 64), 0)
    col_at = lax.broadcasted_iota(jnp.int32, (64, 64), 1)
    upper = jnp.where(col_at >= row_at, full[:, :64], 0.0)
    factor_ref[...] = upper * (1.0 / math.sqrt(256))
    high, low = split2(full[:, 64:] * math.sqrt(256 * 128 * 64))
    left = jnp.concatenate([high, high, low], axis=1)
    for t in range(8):
        high, low = split2(sketch_ref[:, 512 * t : 512 * t + 512])
        right = jnp.concatenate([high, low, high], axis=0)
        basis_ref[:, 512 * t : 512 * t + 512] = jnp.dot(left, right, preferred_element_type=F32)


def params(**more):
    return pltpu.CompilerParams(vmem_limit_bytes=48 * 1024 * 1024, **more)


def whole(space=VMEM):
    return pl.BlockSpec(memory_space=space)


def dma(*shape):
    return pltpu.SemaphoreType.DMA(shape)


def on_device(conductivity, leakage, signs, wells):
    cells = conductivity.shape[0] * conductivity.shape[1]
    probes = signs.shape[0] * GROUP
    count = wells.shape[0]
    wells = wells.reshape(1, count)

    def body(carry):
        turn, _, sketch, _ = carry
        field = VMEM((SPAN, QUADS, 8, 128), F32)
        window = VMEM((SPAN, 2, QUADS, 8, 128), F32)
        sketch, gram, rounds = pl.pallas_call(
            sketch_kernel,
            out_shape=(
                jax.ShapeDtypeStruct(sketch.shape, F32),
                jax.ShapeDtypeStruct((2, 16, 128), F32),
                jax.ShapeDtypeStruct((1,), jnp.int32),
            ),
            in_specs=[whole()] + [whole(pltpu.HBM)] * 4 + [whole()],
            out_specs=(whole(), whole(), whole(SMEM)),
            scratch_shapes=[
                VMEM((1, count), jnp.int32),
                VMEM(conductivity.shape, F32),
                VMEM(leakage.shape, F32),
                VMEM((64, 8, 128), F32),
                VMEM((64, 8, 128), F32),
                window,
                window,
                VMEM((2, CHIPS, probes // GROUP, count), jnp.int32),
                VMEM((7, SPAN, QUADS, 8, 128), F32),
                VMEM((2, SPAN, QUADS, 8, 128), F32),
                field,
                field,
                VMEM((SPAN, 8, QUADS, 128), F32),
                VMEM((SLOTS * QUADS, 128), F32),
                VMEM((256, 128), jnp.bfloat16),
                VMEM((probes, 128), F32),
                VMEM((128, 128), F32),
                VMEM((SLOTS, 128), jnp.int32),
                VMEM((2, 16, 128), F32),
                VMEM((16, 128), F32),
                VMEM((8, 16, 128), F32),
                VMEM((8, 16, 128), F32),
                VMEM((4, 16, 128), F32),
                dma(4),
                dma(2, 4),
                dma(2, 8),
                dma(2),
                dma(SPAN, 8),
                dma(SPAN, 8),
                dma(2, SPAN),
                dma(2),
                dma(2, 8),
                dma(2, 8),
                dma(2, 4),
                dma(2),
            ],
            compiler_params=params(collective_id=0, has_side_effects=True),
            name="sketch",
        )(jnp.broadcast_to(turn, (1, count)), wells, conductivity, leakage, signs, sketch)
        return turn + 1, rounds[0], sketch, gram

    sketch = jnp.zeros((probes, cells // GROUP), F32)
    gram = jnp.zeros((2, 16, 128), F32)
    start = (jnp.int32(0), jnp.int32(1), sketch, gram)
    _, _, sketch, gram = lax.while_loop(lambda carry: carry[0] < carry[1], body, start)
    return pl.pallas_call(
        finish_kernel,
        out_shape=(
            jax.ShapeDtypeStruct((probes, cells // GROUP), F32),
            jax.ShapeDtypeStruct((probes, probes), F32),
        ),
        in_specs=[whole(), whole()],
        out_specs=(whole(), whole()),
        compiler_params=params(),
        name="finish",
    )(gram, sketch)


def solution(mesh):
    placed = (P("space", None), P("space", None), P("probe", None), P())
    return jax.shard_map(
        on_device,
        mesh=mesh,
        in_specs=placed,
        out_specs=(P(None, ("space", "probe")), P()),
        check_vma=False,
    )
```

```python
import functools
import math

import jax
import jax.numpy as jnp
from jax import lax
from jax.experimental import pallas as pl
from jax.experimental.pallas import tpu as pltpu
from jax.sharding import PartitionSpec as P

NZ = 64
SWEEPS = 16
REACH = 2
SPAN = 2 * REACH + 1
GROUP = 16
CHIPS = 8
SLOTS = GROUP * SPAN
ORDER = (2, 1, 3, 0, 4)
EARLY = 3 * GROUP
LATE = SLOTS - EARLY
QUADS = 8
PAIRS = 32

bound_low = 0.005
bound_high = 24.5

F32 = jnp.float32
VMEM = pltpu.VMEM
SMEM = pltpu.SMEM


def chebyshev_table(count):
    center = 0.5 * (bound_high + bound_low)
    spread = 0.5 * (bound_high - bound_low)
    ratio = center / spread
    rho_prev = 1.0 / ratio
    entries = []
    for index_step in range(count):
        rho_next = 1.0 / (2.0 * ratio - rho_prev)
        entries.append((rho_next * rho_prev, 2.0 * rho_next / spread))
        rho_prev = rho_next
    return entries


def start_scale():
    return 1.0 / (0.5 * (bound_high + bound_low))


def decode(cell):
    cell = jnp.maximum(cell, 0)
    x = lax.shift_right_logical(cell, 13)
    y = lax.bitwise_and(lax.shift_right_logical(cell, 6), 127)
    z = lax.bitwise_and(cell, 63)
    y_first = lax.bitwise_and(y + 1, 126 + 128) - 16
    return x, y, y_first, z, z - 15


def lanes(shape=(8, 128)):
    return lax.broadcasted_iota(jnp.int32, shape, 1)


def sublanes(shape=(8, 128)):
    return lax.broadcasted_iota(jnp.int32, shape, 0)


def wrap(shift):
    return lax.bitwise_and(shift, 127)


OFFSETS = (-2, 2, -1, 1)


def barrier_with(partners):
    barrier = pltpu.get_barrier_semaphore()
    for partner in partners:
        pl.semaphore_signal(barrier, inc=1, device_id=partner, device_id_type=pl.DeviceIdType.MESH)
    return lambda: pl.semaphore_wait(barrier, len(partners))


def remote(src, dst, send, recv, device):
    return pltpu.make_async_remote_copy(
        src_ref=src, dst_ref=dst, send_sem=send, recv_sem=recv, device_id=device, device_id_type=pl.DeviceIdType.MESH
    )


def quads(block):
    return range(QUADS) if 0 < block < SPAN - 1 else range(2, 6)


def counted(owner, first, rows):
    shape = (rows, 256)
    lane = lanes(shape)
    ones = jnp.where(jnp.broadcast_to(owner, shape) == sublanes(shape) + first, 1, 0)
    total = ones
    for step in (1, 2, 4, 8, 16, 32, 64, 128):
        total = total + jnp.where(lane >= step, pltpu.roll(total, step, 1), 0)
    return ones, total - ones


def cut(cell, cell_row, e, cond_ref, leak_ref, out_ref):
    pair_first = lax.shift_right_arithmetic(decode(cell)[2], 1)
    shape = (256, 128)
    z_first = decode(jnp.broadcast_to(cell_row, shape))[4]
    row = sublanes(shape)
    lane = lanes(shape)
    same = lax.shift_right_logical(row, 6) == lax.shift_right_logical(lane, 5)
    hit = same & (lax.bitwise_and(row, 63) - z_first == lax.bitwise_and(lane, 31))
    move = jnp.where(hit, 1.0, 0.0).astype(jnp.bfloat16)
    parts = []
    for ref in (cond_ref, leak_ref):
        for k in quads(e):
            one = ref[jnp.clip(pair_first + 2 * k, 0, 63)]
            two = ref[jnp.clip(pair_first + 2 * k + 1, 0, 63)]
            parts.append(jnp.concatenate([one, two], axis=1))
    rows = 8 * len(parts)
    both = jnp.concatenate(split2(jnp.concatenate(parts, axis=0)), axis=0)
    both = jnp.dot(both, move, preferred_element_type=F32)
    both = both[:rows] + both[rows:]
    for n, k in enumerate(quads(e)):
        for prop in range(2):
            at = 8 * (n + prop * len(quads(e)))
            out_ref[e, prop, k] = both[at : at + 8]


def faces(cell, here, blocks, low, high, win_ref, coef):
    _, _, y_first, _, z_first = decode(cell)
    lane = lanes()
    sub = sublanes()
    group = lane // 32
    zz = z_first + lane % 32
    z_ok = (zz >= 0) & (zz < NZ)
    for b in blocks:
        xx = (here + (b - REACH)) * 8 + sub
        x_ok = (xx >= 0) & (xx < 256)
        for k in quads(b):
            yy = y_first + 4 * k + group
            inside = x_ok & (yy >= 0) & (yy < 128) & z_ok
            own = win_ref[b, 0, k]
            before = win_ref[max(b - 1, low), 0, k]
            after = win_ref[min(b + 1, high), 0, k]
            left = win_ref[b, 0, max(k - 1, 0)]
            right = win_ref[b, 0, min(k + 1, QUADS - 1)]
            parts = (
                (jnp.where(sub == 0, pltpu.roll(before, 1, 0), pltpu.roll(own, 1, 0)), xx >= 1),
                (jnp.where(sub == 7, pltpu.roll(after, 7, 0), pltpu.roll(own, 7, 0)), xx < 255),
                (jnp.where(group == 0, pltpu.roll(left, 32, 1), pltpu.roll(own, 32, 1)), yy >= 1),
                (jnp.where(group == 3, pltpu.roll(right, 96, 1), pltpu.roll(own, 96, 1)), yy < 127),
                (pltpu.roll(own, 1, 1), zz >= 1),
                (pltpu.roll(own, 127, 1), zz < NZ - 1),
            )
            diagonal = win_ref[b, 1, k]
            for n, (other, there) in enumerate(parts):
                face = 0.5 * (own + jnp.where(there, other, own))
                diagonal = diagonal + face
                coef[n + 1, b, k] = jnp.where(inside & there, face, 0.0)
            coef[0, b, k] = diagonal


def start_fields(cell, here, search, resid, total):
    x, y, y_first, _, _ = decode(cell)
    lane = lanes()
    sub = sublanes()
    weight = jnp.where(cell >= 0, 1.0, 0.0).astype(F32)
    zero = jnp.zeros((8, 128), F32)
    for b in range(SPAN):
        for k in range(QUADS):
            search[1, b, k] = zero
            if b == REACH and k in (3, 4):
                hit = (sub == x - here * 8) & (4 * k + lane // 32 == y - y_first) & (lane % 32 == 15)
                source = jnp.where(hit, weight, 0.0)
                resid[b, k] = source
                search[0, b, k] = source * start_scale()
            else:
                resid[b, k] = zero
                search[0, b, k] = zero
            total[b, k] = zero


def sweeps(steps, coef, search, resid, total):
    group = lanes() // 32
    sub = sublanes()
    zero = jnp.zeros((8, 128), F32)
    table = chebyshev_table(SWEEPS)
    for j in steps:
        a, c = (float(value) for value in table[j])
        now, later = j % 2, (j + 1) % 2
        wide = j + 1
        k_low, k_high = (15 - wide) // 4, (16 + wide) // 4
        b_low, b_high = (1, 3) if wide <= 8 else (0, 4)
        for b in range(b_low, b_high + 1):
            for k in range(max(k_low, quads(b)[0]), min(k_high, quads(b)[-1]) + 1):
                own = search[now, b, k]
                edge = pltpu.roll(search[now, b - 1, k], 1, 0) if b > 0 else zero
                down = jnp.where(sub == 0, edge, pltpu.roll(own, 1, 0))
                edge = pltpu.roll(search[now, b + 1, k], 7, 0) if b < SPAN - 1 else zero
                up = jnp.where(sub == 7, edge, pltpu.roll(own, 7, 0))
                edge = pltpu.roll(search[now, b, k - 1], 32, 1) if k > 0 else zero
                left = jnp.where(group == 0, edge, pltpu.roll(own, 32, 1))
                edge = pltpu.roll(search[now, b, k + 1], 96, 1) if k < QUADS - 1 else zero
                right = jnp.where(group == 3, edge, pltpu.roll(own, 96, 1))
                image = coef[0, b, k] * own
                image = image - coef[1, b, k] * down
                image = image - coef[2, b, k] * up
                image = image - coef[3, b, k] * left
                image = image - coef[4, b, k] * right
                image = image - coef[5, b, k] * pltpu.roll(own, 1, 1)
                image = image - coef[6, b, k] * pltpu.roll(own, 127, 1)
                rest = resid[b, k] - image
                resid[b, k] = rest
                total[b, k] = total[b, k] + own
                search[later, b, k] = a * own + c * rest


def split2(value):
    high = value.astype(jnp.bfloat16)
    return high, (value - high.astype(F32)).astype(jnp.bfloat16)


def moves(cell):
    shape = (256, 128)
    _, _, y_first, _, z_first = decode(jnp.broadcast_to(cell[0:1, :], shape))
    lane = lanes(shape)
    row = sublanes(shape)
    odd = lax.bitwise_and(lax.shift_right_arithmetic(y_first, 1), 1)
    same_z = lax.bitwise_and(row + z_first, 31) == lax.bitwise_and(lane, 31)
    same_y = lax.bitwise_and(lax.shift_right_logical(row, 5) + 2 * odd, 3) == lax.shift_right_logical(lane, 5)
    hit = same_z & same_y & ((row < 128) == (lane < 64))
    return jnp.where(hit, 1.0, 0.0).astype(jnp.bfloat16)


def align(first, second, b, move, total, out_ref):
    one = split2(jnp.concatenate([total[b, lax.bitwise_and(k - first, 7)] for k in range(QUADS)], axis=0))
    two = split2(jnp.concatenate([total[b, lax.bitwise_and(k - second, 7)] for k in range(QUADS)], axis=0))
    both = jnp.concatenate([jnp.concatenate(part, axis=1) for part in zip(one, two)], axis=0)
    both = jnp.dot(both, move[...], preferred_element_type=F32)
    both = both[:64] + both[64:]
    for k in range(QUADS):
        out_ref[b, :, k, :] = both[8 * k : 8 * k + 8]


def slots(ones, counts, wells, turn, chip):
    shape = (GROUP, 256)
    place = sublanes(shape)
    probe = 2 * lax.bitwise_and(chip - lax.bitwise_and(place, 7), 7) + lax.shift_right_logical(place, 3)
    want = probe + GROUP * jnp.broadcast_to(turn, shape)
    parts = []
    for e in ORDER:
        there = jnp.broadcast_to(ones[e : e + 1], shape) > 0
        parts.append(there & (jnp.broadcast_to(counts[e : e + 1], shape) == want))
    holds = [jnp.where(part, 1.0, 0.0) for part in parts]
    wells = jnp.broadcast_to(wells, shape)
    cells = [jnp.max(jnp.where(part, wells, -1), axis=1, keepdims=True) for part in parts]
    return jnp.concatenate(holds, axis=0), jnp.concatenate(cells, axis=0)


def panel(pick, pair_first, z_first, half, first, number, rows_ref, add):
    pair_first = pair_first - float(PAIRS) * half.astype(F32)
    lane = lanes((number, 128))
    z_here = lane % 64 - z_first[first : first + number]
    shown = (z_here >= 0) & (z_here < 32)
    group = lane // 32
    rest = 64 - number
    for k in range(QUADS):
        own = rows_ref[pl.ds(first * 8 + k, number, stride=8), :]
        r1, r2, r3 = (pltpu.roll(own, 32 * n, 1) for n in (1, 2, 3))
        pairs = (
            jnp.where(group == 0, own, jnp.where(group == 3, r2, r1)),
            jnp.where(group == 0, r2, jnp.where(group == 3, own, r3)),
        )
        for m in range(2):
            high, low = split2(jnp.where(shown, pairs[m], 0.0))
            blank = jnp.zeros((rest, 128), jnp.bfloat16)
            value = jnp.concatenate([high, blank, low, blank], axis=0)
            left = []
            for t in (2 * k + m, 2 * k + m + 16):
                ok = (pair_first <= t) & (t < pair_first + 16)
                left.append(jnp.where(ok, pick, 0.0).astype(jnp.bfloat16))
            both = jnp.dot(jnp.concatenate(left, axis=0), value, preferred_element_type=F32)
            for n in range(2):
                add(128 * (2 * k + m + 16 * n), both[64 * n : 64 * n + 64])


def doubled(value, first, number):
    lane = lanes(value.shape)
    low = pltpu.roll(value, (128 - first) % 128, 1) if first else value
    return jnp.where(lane % 64 < number, jnp.where(lane < 64, low, pltpu.roll(value, (192 - first) % 128, 1)), 0.0)


def gram_of(sketch_ref):
    both = jnp.concatenate(split2(sketch_ref[:64, :]), axis=0)
    full = lax.dot_general(both, both, (((1,), (1,)), ((), ())), preferred_element_type=F32)
    return full[:64, :64] + ((full[:64, 64:] + full[64:, :64]) + full[64:, 64:])


def sketch_kernel(
    turn_ref,
    wells_hbm,
    cond_hbm,
    leak_hbm,
    signs_hbm,
    before_ref,
    sketch_ref,
    rounds_ref,
    wells_ref,
    cond_ref,
    leak_ref,
    cond_pairs,
    leak_pairs,
    cuts,
    win,
    signs,
    coef,
    search,
    resid,
    total,
    fields,
    rows,
    move,
    pick_ref,
    first_ref,
    depth_ref,
    gram_ref,
    mine,
    twin_buf,
    y_buf,
    z_buf,
    x_buf,
    load_sem,
    win_sem,
    sign_sem,
    sign_pair,
    row_send,
    row_recv,
    pair_sem,
    twin_sem,
    y_sem,
    z_sem,
    x_sem,
    last_sem,
):
    count = lax.axis_size("space")
    here = lax.axis_index("space")
    me = lax.axis_index("probe")
    chip = me // 2
    core = me % 2
    x = here // 8
    z = here % 8
    near = [(lax.rem(here + d + count, count), me) for d in OFFSETS]
    along = [(here, lax.rem(chip + r, CHIPS) * 2 + core) for r in range(1, CHIPS)]
    ring_z = [(x * 8 + lax.rem(z + r, 8), me) for r in range(1, 8)]
    ring_x = [(lax.rem(x + r, 4) * 8 + z, me) for r in range(1, 4)]
    twin = (here, chip * 2 + 1 - core)
    entered = barrier_with(near + along + [twin] + ring_z + ring_x)
    loads = []
    pieces = ((wells_hbm, wells_ref), (cond_hbm, cond_ref), (leak_hbm, leak_ref), (signs_hbm, signs.at[core, chip]))
    for i, (src, dst) in enumerate(pieces):
        loads.append(pltpu.make_async_copy(src, dst, load_sem.at[i]))
        loads[-1].start()
    one = jnp.ones((8, 128), F32)
    for b in (0, SPAN - 1):
        for k in range(QUADS):
            if k not in quads(b):
                win[b, 0, k] = one
    loads[0].wait()
    wells = wells_ref[...]
    turn = turn_ref[...]
    owner = lax.shift_right_logical(wells, 16)
    ones, counts = counted(owner, here - REACH, 8)
    chosen = (ones > 0) & (counts == me + GROUP * jnp.broadcast_to(turn, (8, 256)))
    cells = jnp.max(jnp.where(chosen, jnp.broadcast_to(wells, (8, 256)), -1), axis=1, keepdims=True)
    cell = jnp.broadcast_to(cells[REACH : REACH + 1], (8, 128))
    for copy in loads[1:]:
        copy.wait()
    for src, dst in ((cond_ref, cond_pairs), (leak_ref, leak_pairs)):
        for t in range(64):
            dst[t] = src[:, 128 * t : 128 * t + 128]
    for e in range(SPAN):
        cut(cells[e, 0], cells[e : e + 1], e, cond_pairs, leak_pairs, cuts)
    entered()
    sent = []
    windows = []
    for i, d in enumerate(OFFSETS):
        src, dst = cuts.at[d + 2], win.at[2 - d]
        if d in (-2, 2):
            src, dst = cuts.at[d + 2, :, pl.ds(2, 4)], win.at[2 - d, :, pl.ds(2, 4)]
        copy = remote(src, dst, win_sem.at[0, i], win_sem.at[1, i], near[i])
        copy.start()
        windows.append(copy)
    shared = []
    for r in range(1, CHIPS):
        part = signs.at[core, chip]
        copy = remote(part, part, sign_sem.at[0, r], sign_sem.at[1, r], along[r - 1])
        copy.start()
        shared.append(copy)
    win[REACH] = cuts[REACH]
    start_fields(cell, here, search, resid, total)
    move[...] = moves(cell)
    all_ones, all_counts = counted(owner, 0, count)
    rounds_ref[0] = lax.shift_right_logical(jnp.max(jnp.where(all_ones > 0, all_counts, 0)), 4) + 1
    holds, slot_cells = slots(ones, counts, wells, turn, chip)
    _, _, y_first, _, z_first = decode(jnp.broadcast_to(slot_cells, (SLOTS, 128)))
    depth_ref[...] = z_first
    pairs_first = lax.shift_right_arithmetic(y_first, 1).astype(F32)
    pairs_first = jnp.concatenate([pairs_first, jnp.zeros((128 - SLOTS, 128), F32)], axis=0)
    pairs_first = pairs_first.T
    for copy in windows[2:]:
        copy.wait_recv()
    faces(cell, here, (1, 2, 3), 1, 3, win, coef)
    sweeps(range(8), coef, search, resid, total)
    for copy in windows[:2]:
        copy.wait_recv()
    faces(cell, here, (0, 1, 3, 4), 0, 4, win, coef)
    sweeps(range(8, SWEEPS - 1), coef, search, resid, total)
    last = (SWEEPS - 1) % 2
    for b in range(SPAN):
        for k in range(QUADS):
            total[b, k] = total[b, k] + search[last, b, k]
    y_first = decode(cells[REACH, 0])[2]
    second = lax.shift_right_arithmetic(y_first, 2)
    first = second + lax.bitwise_and(lax.shift_right_arithmetic(y_first, 1), 1)
    arrivals = {}
    for d in OFFSETS + (0,):
        align(first, second, d + 2, move, total, fields)
        e = 2 - d
        for r in (4, 3, 5, 2, 6, 1, 7, 0):
            target = lax.rem(chip + r, CHIPS)
            place = rows.at[pl.ds(pl.multiple_of((ORDER.index(e) * GROUP + core * CHIPS + r) * 8, 8), 8)]
            if d == 0 and r == 0:
                rows[pl.ds(pl.multiple_of((ORDER.index(e) * GROUP + core * CHIPS) * 8, 8), 8), :] = fields[REACH, chip]
                continue
            device = (lax.rem(here + d + count, count), target * 2 + core)
            copy = remote(fields.at[d + 2, target], place, row_send.at[d + 2, r], row_recv.at[e, r], device)
            copy.start()
            arrivals[e, r] = copy
    for copy in shared:
        copy.wait_recv()
    pair = remote(signs.at[core], signs.at[core], sign_pair.at[0], sign_pair.at[1], twin)
    pair.start()
    pair.wait_recv()
    table = jnp.concatenate([signs[p % 2, p // 2] for p in range(GROUP)], axis=0)
    table = (2 * table - 1).astype(F32).astype(jnp.bfloat16)
    holds = jnp.concatenate([holds, jnp.zeros((128 - SLOTS, 256), F32)], axis=0).astype(jnp.bfloat16)
    pick = lax.dot_general(table, holds, (((1,), (1,)), ((), ())), preferred_element_type=F32)
    keep = jnp.where(turn[:, :128] > 0, 1.0, 0.0)
    parts = ((0, EARLY), (EARLY, LATE))
    for n, (start, number) in enumerate(parts):
        pick_ref[n] = doubled(pick, start, number)
        first_ref[n] = doubled(pairs_first[0:8], start, number)

    def put(at, value):
        sketch_ref[:64, at : at + 128] = value + keep * before_ref[:64, at : at + 128]

    def add(at, value):
        sketch_ref[:64, at : at + 128] = sketch_ref[:64, at : at + 128] + value

    pairs = []
    for e in ORDER:
        for r in range(CHIPS):
            if (e, r) != (REACH, 0):
                arrivals[e, r].wait_recv()
        part = rows.at[pl.ds(pl.multiple_of((ORDER.index(e) * GROUP + core * CHIPS) * 8, 8), 8 * CHIPS)]
        copy = remote(part, part, pair_sem.at[0, e], pair_sem.at[1, e], twin)
        copy.start()
        pairs.append(copy)
        if e == 3:
            for copy in pairs:
                copy.wait_recv()
            panel(pick_ref[0], first_ref[0, 0:1, :], depth_ref[...], core, 0, EARLY, rows, put)
    for copy in pairs[3:]:
        copy.wait_recv()
    panel(pick_ref[1], first_ref[1, 0:1, :], depth_ref[...], core, EARLY, LATE, rows, add)
    sent += windows + shared + [pair] + list(arrivals.values()) + pairs
    gram = gram_of(sketch_ref)
    for h in range(2):
        mine[h] = jnp.concatenate([gram[32 * h : 32 * h + 16], gram[32 * h + 16 : 32 * h + 32]], axis=1)
    copy = remote(mine.at[1 - core], twin_buf, twin_sem.at[0], twin_sem.at[1], twin)
    copy.start()
    sent.append(copy)
    copy.wait_recv()
    value = mine[core] + twin_buf[...]
    for buf, sem, at, ring in ((y_buf, y_sem, chip, along), (z_buf, z_sem, z, ring_z), (x_buf, x_sem, x, ring_x)):
        buf[at] = value
        steps = []
        for r, device in enumerate(ring):
            copy = remote(buf.at[at], buf.at[at], sem.at[0, r], sem.at[1, r], device)
            copy.start()
            steps.append(copy)
        for copy in steps:
            copy.wait_recv()
        sent += steps
        value = buf[0]
        for r in range(1, len(ring) + 1):
            value = value + buf[r]
    gram_ref[core] = value
    copy = remote(gram_ref.at[core], gram_ref.at[core], last_sem.at[0], last_sem.at[1], twin)
    copy.start()
    copy.wait_recv()
    for h in range(2):
        sketch_ref[64:, 128 * h : 128 * h + 128] = gram_ref[h]
    for item in sent + [copy]:
        item.wait_send()


def finish_kernel(sketch_ref, basis_ref, factor_ref):
    shape = (8, 128)
    lane = lanes(shape)
    sub = sublanes(shape)
    rows = []
    for i in range(8):
        at = 128 * (i // 4)
        block = sketch_ref[64 + 8 * (i % 2) : 72 + 8 * (i % 2), at : at + 128]
        if i % 4 >= 2:
            block = pltpu.roll(block, 64, 1)
        rows.append(jnp.where(lane < 64, block, jnp.where(lane - 64 == sub + 8 * i, 1.0, 0.0)))
    for n in range(8):
        columns = [[jnp.broadcast_to(rows[i][:, 8 * n + c : 8 * n + c + 1], shape) for i in range(n, 8)] for c in range(8)]
        own = rows[n]
        lines = []
        for c in range(8):
            pivot = jnp.broadcast_to(columns[c][0][c : c + 1, :], shape)
            scale = lax.rsqrt(pivot)
            scale = scale * (1.5 - 0.5 * pivot * scale * scale)
            line = jnp.broadcast_to(own[c : c + 1, :], shape) * scale
            columns[c] = [value * scale for value in columns[c]]
            below = jnp.where(sub > c, columns[c][0], 0.0)
            own = jnp.where(sub == c, line, own - below * line)
            for later in range(c + 1, 8):
                factor = jnp.broadcast_to(columns[c][0][later : later + 1, :], shape)
                columns[later][0] = columns[later][0] - below * factor
                for i in range(1, 8 - n):
                    columns[later][i] = columns[later][i] - columns[c][i] * factor
            lines.append(line)
        rows[n] = own
        for i in range(n + 1, 8):
            value = rows[i]
            for c in range(8):
                value = value - columns[c][i - n] * lines[c]
            rows[i] = value
    full = jnp.concatenate(rows, axis=0)
    row_at = lax.broadcasted_iota(jnp.int32, (64, 64), 0)
    col_at = lax.broadcasted_iota(jnp.int32, (64, 64), 1)
    upper = jnp.where(col_at >= row_at, full[:, :64], 0.0)
    factor_ref[...] = upper * (1.0 / math.sqrt(256))
    high, low = split2(full[:, 64:] * math.sqrt(256 * 128 * 64))
    left = jnp.concatenate([high, high, low], axis=1)
    for t in range(8):
        high, low = split2(sketch_ref[:64, 512 * t : 512 * t + 512])
        right = jnp.concatenate([high, low, high], axis=0)
        basis_ref[:, 512 * t : 512 * t + 512] = jnp.dot(left, right, preferred_element_type=F32)


def params(**more):
    return pltpu.CompilerParams(vmem_limit_bytes=48 * 1024 * 1024, **more)


def whole(space=VMEM):
    return pl.BlockSpec(memory_space=space)


def dma(*shape):
    return pltpu.SemaphoreType.DMA(shape)


def on_device(conductivity, leakage, signs, wells):
    cells = conductivity.shape[0] * conductivity.shape[1]
    probes = signs.shape[0] * GROUP
    count = wells.shape[0]
    wells = wells.reshape(1, count)

    def body(carry):
        turn, _, sketch = carry
        field = VMEM((SPAN, QUADS, 8, 128), F32)
        window = VMEM((SPAN, 2, QUADS, 8, 128), F32)
        sketch, rounds = pl.pallas_call(
            sketch_kernel,
            out_shape=(
                jax.ShapeDtypeStruct(sketch.shape, F32),
                jax.ShapeDtypeStruct((1,), jnp.int32),
            ),
            in_specs=[whole()] + [whole(pltpu.HBM)] * 4 + [whole()],
            out_specs=(whole(), whole(SMEM)),
            scratch_shapes=[
                VMEM((1, count), jnp.int32),
                VMEM(conductivity.shape, F32),
                VMEM(leakage.shape, F32),
                VMEM((64, 8, 128), F32),
                VMEM((64, 8, 128), F32),
                window,
                window,
                VMEM((2, CHIPS, probes // GROUP, count), jnp.int32),
                VMEM((7, SPAN, QUADS, 8, 128), F32),
                VMEM((2, SPAN, QUADS, 8, 128), F32),
                field,
                field,
                VMEM((SPAN, 8, QUADS, 128), F32),
                VMEM((SLOTS * QUADS, 128), F32),
                VMEM((256, 128), jnp.bfloat16),
                VMEM((2, probes, 128), F32),
                VMEM((2, 8, 128), F32),
                VMEM((SLOTS, 128), jnp.int32),
                VMEM((2, 16, 128), F32),
                VMEM((2, 16, 128), F32),
                VMEM((16, 128), F32),
                VMEM((8, 16, 128), F32),
                VMEM((8, 16, 128), F32),
                VMEM((4, 16, 128), F32),
                dma(4),
                dma(2, 4),
                dma(2, 8),
                dma(2),
                dma(SPAN, 8),
                dma(SPAN, 8),
                dma(2, SPAN),
                dma(2),
                dma(2, 8),
                dma(2, 8),
                dma(2, 4),
                dma(2),
            ],
            compiler_params=params(collective_id=0, has_side_effects=True),
            name="sketch",
        )(jnp.broadcast_to(turn, (1, count)), wells, conductivity, leakage, signs, sketch)
        return turn + 1, rounds[0], sketch

    sketch = jnp.zeros((probes + 16, cells // GROUP), F32)
    start = (jnp.int32(0), jnp.int32(1), sketch)
    _, _, sketch = lax.while_loop(lambda carry: carry[0] < carry[1], body, start)
    return pl.pallas_call(
        finish_kernel,
        out_shape=(
            jax.ShapeDtypeStruct((probes, cells // GROUP), F32),
            jax.ShapeDtypeStruct((probes, probes), F32),
        ),
        in_specs=[whole()],
        out_specs=(whole(), whole()),
        compiler_params=params(),
        name="finish",
    )(sketch)


def solution(mesh):
    placed = (P("space", None), P("space", None), P("probe", None), P())
    return jax.shard_map(
        on_device,
        mesh=mesh,
        in_specs=placed,
        out_specs=(P(None, ("space", "probe")), P()),
        check_vma=False,
    )
```

```python
import functools
import math

import jax
import jax.numpy as jnp
from jax import lax
from jax.experimental import pallas as pl
from jax.experimental.pallas import tpu as pltpu
from jax.sharding import PartitionSpec as P

NZ = 64
SWEEPS = 16
REACH = 2
SPAN = 2 * REACH + 1
GROUP = 16
CHIPS = 8
SLOTS = GROUP * SPAN
ORDER = (2, 1, 3, 0, 4)
EARLY = 3 * GROUP
LATE = SLOTS - EARLY
QUADS = 8
PAIRS = 32

bound_low = 0.005
bound_high = 24.5

F32 = jnp.float32
VMEM = pltpu.VMEM
SMEM = pltpu.SMEM


def chebyshev_table(count):
    center = 0.5 * (bound_high + bound_low)
    spread = 0.5 * (bound_high - bound_low)
    ratio = center / spread
    rho_prev = 1.0 / ratio
    entries = []
    for index_step in range(count):
        rho_next = 1.0 / (2.0 * ratio - rho_prev)
        entries.append((rho_next * rho_prev, 2.0 * rho_next / spread))
        rho_prev = rho_next
    return entries


def start_scale():
    return 1.0 / (0.5 * (bound_high + bound_low))


def decode(cell):
    cell = jnp.maximum(cell, 0)
    x = lax.shift_right_logical(cell, 13)
    y = lax.bitwise_and(lax.shift_right_logical(cell, 6), 127)
    z = lax.bitwise_and(cell, 63)
    y_first = lax.bitwise_and(y + 1, 126 + 128) - 16
    return x, y, y_first, z, z - 15


def lanes(shape=(8, 128)):
    return lax.broadcasted_iota(jnp.int32, shape, 1)


def sublanes(shape=(8, 128)):
    return lax.broadcasted_iota(jnp.int32, shape, 0)


def wrap(shift):
    return lax.bitwise_and(shift, 127)


OFFSETS = (-2, 2, -1, 1)


def barrier_with(partners):
    barrier = pltpu.get_barrier_semaphore()
    for partner in partners:
        pl.semaphore_signal(barrier, inc=1, device_id=partner, device_id_type=pl.DeviceIdType.MESH)
    return lambda: pl.semaphore_wait(barrier, len(partners))


def remote(src, dst, send, recv, device):
    return pltpu.make_async_remote_copy(
        src_ref=src, dst_ref=dst, send_sem=send, recv_sem=recv, device_id=device, device_id_type=pl.DeviceIdType.MESH
    )


def quads(block):
    return range(QUADS) if 0 < block < SPAN - 1 else range(2, 6)


def counted(owner, first, rows):
    shape = (rows, 256)
    lane = lanes(shape)
    ones = jnp.where(jnp.broadcast_to(owner, shape) == sublanes(shape) + first, 1, 0)
    total = ones
    for step in (1, 2, 4, 8, 16, 32, 64, 128):
        total = total + jnp.where(lane >= step, pltpu.roll(total, step, 1), 0)
    return ones, total - ones


def cut(cell, cell_row, e, cond_ref, leak_ref, out_ref):
    pair_first = lax.shift_right_arithmetic(decode(cell)[2], 1)
    shape = (256, 128)
    z_first = decode(jnp.broadcast_to(cell_row, shape))[4]
    row = sublanes(shape)
    lane = lanes(shape)
    same = lax.shift_right_logical(row, 6) == lax.shift_right_logical(lane, 5)
    hit = same & (lax.bitwise_and(row, 63) - z_first == lax.bitwise_and(lane, 31))
    move = jnp.where(hit, 1.0, 0.0).astype(jnp.bfloat16)
    parts = []
    for ref in (cond_ref, leak_ref):
        for k in quads(e):
            one = ref[jnp.clip(pair_first + 2 * k, 0, 63)]
            two = ref[jnp.clip(pair_first + 2 * k + 1, 0, 63)]
            parts.append(jnp.concatenate([one, two], axis=1))
    rows = 8 * len(parts)
    both = jnp.concatenate(split2(jnp.concatenate(parts, axis=0)), axis=0)
    both = jnp.dot(both, move, preferred_element_type=F32)
    both = both[:rows] + both[rows:]
    for n, k in enumerate(quads(e)):
        for prop in range(2):
            at = 8 * (n + prop * len(quads(e)))
            out_ref[e, prop, k] = both[at : at + 8]


def faces(cell, here, blocks, low, high, win_ref, coef):
    _, _, y_first, _, z_first = decode(cell)
    lane = lanes()
    sub = sublanes()
    group = lane // 32
    zz = z_first + lane % 32
    z_ok = (zz >= 0) & (zz < NZ)
    for b in blocks:
        xx = (here + (b - REACH)) * 8 + sub
        x_ok = (xx >= 0) & (xx < 256)
        for k in quads(b):
            yy = y_first + 4 * k + group
            inside = x_ok & (yy >= 0) & (yy < 128) & z_ok
            own = win_ref[b, 0, k]
            before = win_ref[max(b - 1, low), 0, k]
            after = win_ref[min(b + 1, high), 0, k]
            left = win_ref[b, 0, max(k - 1, 0)]
            right = win_ref[b, 0, min(k + 1, QUADS - 1)]
            parts = (
                (jnp.where(sub == 0, pltpu.roll(before, 1, 0), pltpu.roll(own, 1, 0)), xx >= 1),
                (jnp.where(sub == 7, pltpu.roll(after, 7, 0), pltpu.roll(own, 7, 0)), xx < 255),
                (jnp.where(group == 0, pltpu.roll(left, 32, 1), pltpu.roll(own, 32, 1)), yy >= 1),
                (jnp.where(group == 3, pltpu.roll(right, 96, 1), pltpu.roll(own, 96, 1)), yy < 127),
                (pltpu.roll(own, 1, 1), zz >= 1),
                (pltpu.roll(own, 127, 1), zz < NZ - 1),
            )
            diagonal = win_ref[b, 1, k]
            for n, (other, there) in enumerate(parts):
                face = 0.5 * (own + jnp.where(there, other, own))
                diagonal = diagonal + face
                coef[n + 1, b, k] = jnp.where(inside & there, face, 0.0)
            coef[0, b, k] = diagonal


def start_fields(cell, here, search, resid, total):
    x, y, y_first, _, _ = decode(cell)
    lane = lanes()
    sub = sublanes()
    weight = jnp.where(cell >= 0, 1.0, 0.0).astype(F32)
    zero = jnp.zeros((8, 128), F32)
    for b in range(SPAN):
        for k in range(QUADS):
            search[1, b, k] = zero
            if b == REACH and k in (3, 4):
                hit = (sub == x - here * 8) & (4 * k + lane // 32 == y - y_first) & (lane % 32 == 15)
                source = jnp.where(hit, weight, 0.0)
                resid[b, k] = source
                search[0, b, k] = source * start_scale()
            else:
                resid[b, k] = zero
                search[0, b, k] = zero
            total[b, k] = zero


def sweeps(steps, coef, search, resid, total):
    group = lanes() // 32
    sub = sublanes()
    zero = jnp.zeros((8, 128), F32)
    table = chebyshev_table(SWEEPS)
    for j in steps:
        a, c = (float(value) for value in table[j])
        now, later = j % 2, (j + 1) % 2
        wide = j + 1
        k_low, k_high = (15 - wide) // 4, (16 + wide) // 4
        b_low, b_high = (1, 3) if wide <= 8 else (0, 4)
        for b in range(b_low, b_high + 1):
            for k in range(max(k_low, quads(b)[0]), min(k_high, quads(b)[-1]) + 1):
                own = search[now, b, k]
                edge = pltpu.roll(search[now, b - 1, k], 1, 0) if b > 0 else zero
                down = jnp.where(sub == 0, edge, pltpu.roll(own, 1, 0))
                edge = pltpu.roll(search[now, b + 1, k], 7, 0) if b < SPAN - 1 else zero
                up = jnp.where(sub == 7, edge, pltpu.roll(own, 7, 0))
                edge = pltpu.roll(search[now, b, k - 1], 32, 1) if k > 0 else zero
                left = jnp.where(group == 0, edge, pltpu.roll(own, 32, 1))
                edge = pltpu.roll(search[now, b, k + 1], 96, 1) if k < QUADS - 1 else zero
                right = jnp.where(group == 3, edge, pltpu.roll(own, 96, 1))
                image = coef[0, b, k] * own
                image = image - coef[1, b, k] * down
                image = image - coef[2, b, k] * up
                image = image - coef[3, b, k] * left
                image = image - coef[4, b, k] * right
                image = image - coef[5, b, k] * pltpu.roll(own, 1, 1)
                image = image - coef[6, b, k] * pltpu.roll(own, 127, 1)
                rest = resid[b, k] - image
                resid[b, k] = rest
                total[b, k] = total[b, k] + own
                search[later, b, k] = a * own + c * rest


def split2(value):
    high = value.astype(jnp.bfloat16)
    return high, (value - high.astype(F32)).astype(jnp.bfloat16)


def moves(cell):
    shape = (256, 128)
    _, _, y_first, _, z_first = decode(jnp.broadcast_to(cell[0:1, :], shape))
    lane = lanes(shape)
    row = sublanes(shape)
    odd = lax.bitwise_and(lax.shift_right_arithmetic(y_first, 1), 1)
    same_z = lax.bitwise_and(row + z_first, 31) == lax.bitwise_and(lane, 31)
    same_y = lax.bitwise_and(lax.shift_right_logical(row, 5) + 2 * odd, 3) == lax.shift_right_logical(lane, 5)
    hit = same_z & same_y & ((row < 128) == (lane < 64))
    return jnp.where(hit, 1.0, 0.0).astype(jnp.bfloat16)


def align(first, second, b, move, total, out_ref):
    one = split2(jnp.concatenate([total[b, lax.bitwise_and(k - first, 7)] for k in range(QUADS)], axis=0))
    two = split2(jnp.concatenate([total[b, lax.bitwise_and(k - second, 7)] for k in range(QUADS)], axis=0))
    both = jnp.concatenate([jnp.concatenate(part, axis=1) for part in zip(one, two)], axis=0)
    both = jnp.dot(both, move[...], preferred_element_type=F32)
    both = both[:64] + both[64:]
    for k in range(QUADS):
        out_ref[b, :, k, :] = both[8 * k : 8 * k + 8]


def slots(ones, counts, wells, turn, chip):
    shape = (GROUP, 256)
    place = sublanes(shape)
    probe = 2 * lax.bitwise_and(chip - lax.bitwise_and(place, 7), 7) + lax.shift_right_logical(place, 3)
    want = probe + GROUP * jnp.broadcast_to(turn, shape)
    parts = []
    for e in ORDER:
        there = jnp.broadcast_to(ones[e : e + 1], shape) > 0
        parts.append(there & (jnp.broadcast_to(counts[e : e + 1], shape) == want))
    holds = [jnp.where(part, 1.0, 0.0) for part in parts]
    wells = jnp.broadcast_to(wells, shape)
    cells = [jnp.max(jnp.where(part, wells, -1), axis=1, keepdims=True) for part in parts]
    return jnp.concatenate(holds, axis=0), jnp.concatenate(cells, axis=0)


def panel(pick, pair_first, z_first, half, first, number, rows_ref, add):
    pair_first = pair_first - float(PAIRS) * half.astype(F32)
    lane = lanes((number, 128))
    z_here = lane % 64 - z_first[first : first + number]
    shown = (z_here >= 0) & (z_here < 32)
    group = lane // 32
    rest = 64 - number
    for k in range(QUADS):
        own = rows_ref[pl.ds(first * 8 + k, number, stride=8), :]
        r1, r2, r3 = (pltpu.roll(own, 32 * n, 1) for n in (1, 2, 3))
        pairs = (
            jnp.where(group == 0, own, jnp.where(group == 3, r2, r1)),
            jnp.where(group == 0, r2, jnp.where(group == 3, own, r3)),
        )
        for m in range(2):
            high, low = split2(jnp.where(shown, pairs[m], 0.0))
            blank = jnp.zeros((rest, 128), jnp.bfloat16)
            value = jnp.concatenate([high, blank, low, blank], axis=0)
            left = []
            for t in (2 * k + m, 2 * k + m + 16):
                ok = (pair_first <= t) & (t < pair_first + 16)
                left.append(jnp.where(ok, pick, 0.0).astype(jnp.bfloat16))
            both = jnp.dot(jnp.concatenate(left, axis=0), value, preferred_element_type=F32)
            for n in range(2):
                add(128 * (2 * k + m + 16 * n), both[64 * n : 64 * n + 64])


def doubled(value, first, number):
    lane = lanes(value.shape)
    low = pltpu.roll(value, (128 - first) % 128, 1) if first else value
    return jnp.where(lane % 64 < number, jnp.where(lane < 64, low, pltpu.roll(value, (192 - first) % 128, 1)), 0.0)


def gram_of(sketch_ref):
    both = jnp.concatenate(split2(sketch_ref[:64, :]), axis=0)
    full = lax.dot_general(both, both, (((1,), (1,)), ((), ())), preferred_element_type=F32)
    return full[:64, :64] + ((full[:64, 64:] + full[64:, :64]) + full[64:, 64:])


def sketch_kernel(
    turn_ref,
    wells_hbm,
    cond_hbm,
    leak_hbm,
    signs_hbm,
    before_ref,
    sketch_ref,
    rounds_ref,
    wells_ref,
    cond_ref,
    leak_ref,
    cond_pairs,
    leak_pairs,
    cuts,
    win,
    signs,
    coef,
    search,
    resid,
    total,
    fields,
    rows,
    move,
    pick_ref,
    first_ref,
    depth_ref,
    mine,
    twin_buf,
    y_buf,
    z_buf,
    x_buf,
    load_sem,
    win_sem,
    sign_sem,
    sign_pair,
    row_send,
    row_recv,
    pair_sem,
    twin_sem,
    y_sem,
    z_sem,
    x_sem,
):
    count = lax.axis_size("space")
    here = lax.axis_index("space")
    me = lax.axis_index("probe")
    chip = me // 2
    core = me % 2
    x = here // 8
    z = here % 8
    near = [(lax.rem(here + d + count, count), me) for d in OFFSETS]
    along = [(here, lax.rem(chip + r, CHIPS) * 2 + core) for r in range(1, CHIPS)]
    ring_z = [(x * 8 + lax.rem(z + r, 8), me) for r in range(1, 8)]
    ring_x = [(lax.rem(x + r, 4) * 8 + z, me) for r in range(1, 4)]
    twin = (here, chip * 2 + 1 - core)
    entered = barrier_with(near + along + [twin] + ring_z + ring_x)
    loads = []
    pieces = ((wells_hbm, wells_ref), (cond_hbm, cond_ref), (leak_hbm, leak_ref), (signs_hbm, signs.at[core, chip]))
    for i, (src, dst) in enumerate(pieces):
        loads.append(pltpu.make_async_copy(src, dst, load_sem.at[i]))
        loads[-1].start()
    one = jnp.ones((8, 128), F32)
    for b in (0, SPAN - 1):
        for k in range(QUADS):
            if k not in quads(b):
                win[b, 0, k] = one
    loads[0].wait()
    wells = wells_ref[...]
    turn = turn_ref[...]
    owner = lax.shift_right_logical(wells, 16)
    ones, counts = counted(owner, here - REACH, 8)
    chosen = (ones > 0) & (counts == me + GROUP * jnp.broadcast_to(turn, (8, 256)))
    cells = jnp.max(jnp.where(chosen, jnp.broadcast_to(wells, (8, 256)), -1), axis=1, keepdims=True)
    cell = jnp.broadcast_to(cells[REACH : REACH + 1], (8, 128))
    for copy in loads[1:]:
        copy.wait()
    for src, dst in ((cond_ref, cond_pairs), (leak_ref, leak_pairs)):
        for t in range(64):
            dst[t] = src[:, 128 * t : 128 * t + 128]
    for e in range(SPAN):
        cut(cells[e, 0], cells[e : e + 1], e, cond_pairs, leak_pairs, cuts)
    entered()
    sent = []
    windows = []
    for i, d in enumerate(OFFSETS):
        src, dst = cuts.at[d + 2], win.at[2 - d]
        if d in (-2, 2):
            src, dst = cuts.at[d + 2, :, pl.ds(2, 4)], win.at[2 - d, :, pl.ds(2, 4)]
        copy = remote(src, dst, win_sem.at[0, i], win_sem.at[1, i], near[i])
        copy.start()
        windows.append(copy)
    win[REACH] = cuts[REACH]
    start_fields(cell, here, search, resid, total)
    move[...] = moves(cell)
    all_ones, all_counts = counted(owner, 0, count)
    rounds_ref[0] = lax.shift_right_logical(jnp.max(jnp.where(all_ones > 0, all_counts, 0)), 4) + 1
    holds, slot_cells = slots(ones, counts, wells, turn, chip)
    _, _, y_first, _, z_first = decode(jnp.broadcast_to(slot_cells, (SLOTS, 128)))
    depth_ref[...] = z_first
    pairs_first = lax.shift_right_arithmetic(y_first, 1).astype(F32)
    pairs_first = jnp.concatenate([pairs_first, jnp.zeros((128 - SLOTS, 128), F32)], axis=0)
    pairs_first = pairs_first.T
    for copy in windows[2:]:
        copy.wait_recv()
    shared = []
    for r in range(1, CHIPS):
        part = signs.at[core, chip]
        copy = remote(part, part, sign_sem.at[0, r], sign_sem.at[1, r], along[r - 1])
        copy.start()
        shared.append(copy)
    faces(cell, here, (1, 2, 3), 1, 3, win, coef)
    sweeps(range(8), coef, search, resid, total)
    for copy in windows[:2]:
        copy.wait_recv()
    faces(cell, here, (0, 1, 3, 4), 0, 4, win, coef)
    sweeps(range(8, SWEEPS - 1), coef, search, resid, total)
    last = (SWEEPS - 1) % 2
    for b in range(SPAN):
        for k in range(QUADS):
            total[b, k] = total[b, k] + search[last, b, k]
    y_first = decode(cells[REACH, 0])[2]
    second = lax.shift_right_arithmetic(y_first, 2)
    first = second + lax.bitwise_and(lax.shift_right_arithmetic(y_first, 1), 1)
    arrivals = {}
    for d in OFFSETS + (0,):
        align(first, second, d + 2, move, total, fields)
        e = 2 - d
        for r in (4, 3, 5, 2, 6, 1, 7, 0):
            target = lax.rem(chip + r, CHIPS)
            place = rows.at[pl.ds(pl.multiple_of((ORDER.index(e) * GROUP + core * CHIPS + r) * 8, 8), 8)]
            if d == 0 and r == 0:
                rows[pl.ds(pl.multiple_of((ORDER.index(e) * GROUP + core * CHIPS) * 8, 8), 8), :] = fields[REACH, chip]
                continue
            device = (lax.rem(here + d + count, count), target * 2 + core)
            copy = remote(fields.at[d + 2, target], place, row_send.at[d + 2, r], row_recv.at[e, r], device)
            copy.start()
            arrivals[e, r] = copy
    for copy in shared:
        copy.wait_recv()
    pair = remote(signs.at[core], signs.at[core], sign_pair.at[0], sign_pair.at[1], twin)
    pair.start()
    pair.wait_recv()
    table = jnp.concatenate([signs[p % 2, p // 2] for p in range(GROUP)], axis=0)
    table = (2 * table - 1).astype(F32).astype(jnp.bfloat16)
    holds = jnp.concatenate([holds, jnp.zeros((128 - SLOTS, 256), F32)], axis=0).astype(jnp.bfloat16)
    pick = lax.dot_general(table, holds, (((1,), (1,)), ((), ())), preferred_element_type=F32)
    keep = jnp.where(turn[:, :128] > 0, 1.0, 0.0)
    parts = ((0, EARLY), (EARLY, LATE))
    for n, (start, number) in enumerate(parts):
        pick_ref[n] = doubled(pick, start, number)
        first_ref[n] = doubled(pairs_first[0:8], start, number)

    def put(at, value):
        sketch_ref[:64, at : at + 128] = value + keep * before_ref[:64, at : at + 128]

    def add(at, value):
        sketch_ref[:64, at : at + 128] = sketch_ref[:64, at : at + 128] + value

    pairs = []
    for e in ORDER:
        for r in range(CHIPS):
            if (e, r) != (REACH, 0):
                arrivals[e, r].wait_recv()
        part = rows.at[pl.ds(pl.multiple_of((ORDER.index(e) * GROUP + core * CHIPS) * 8, 8), 8 * CHIPS)]
        copy = remote(part, part, pair_sem.at[0, e], pair_sem.at[1, e], twin)
        copy.start()
        pairs.append(copy)
        if e == 3:
            for copy in pairs:
                copy.wait_recv()
            panel(pick_ref[0], first_ref[0, 0:1, :], depth_ref[...], core, 0, EARLY, rows, put)
    for copy in pairs[3:]:
        copy.wait_recv()
    panel(pick_ref[1], first_ref[1, 0:1, :], depth_ref[...], core, EARLY, LATE, rows, add)
    sent += windows + shared + [pair] + list(arrivals.values()) + pairs
    gram = gram_of(sketch_ref)
    for h in range(2):
        mine[h] = jnp.concatenate([gram[32 * h : 32 * h + 16], gram[32 * h + 16 : 32 * h + 32]], axis=1)
    copy = remote(mine.at[1 - core], twin_buf, twin_sem.at[0], twin_sem.at[1], twin)
    copy.start()
    sent.append(copy)
    copy.wait_recv()
    value = mine[core] + twin_buf[...]
    for buf, sem, at, ring in ((y_buf, y_sem, chip, along), (z_buf, z_sem, z, ring_z)):
        buf[at] = value
        steps = []
        for r, device in sorted(enumerate(ring), key=lambda item: abs(2 * item[0] + 1 - len(ring))):
            copy = remote(buf.at[at], buf.at[at], sem.at[0, r], sem.at[1, r], device)
            copy.start()
            steps.append(copy)
        for copy in steps:
            copy.wait_recv()
        sent += steps
        value = buf[0]
        for r in range(1, 8):
            value = value + buf[r]
    x_buf[core, x] = value
    steps = []
    for r in (2, 1, 3, 0):
        for other in range(2):
            if r == 0 and other == 0:
                continue
            device = (lax.rem(x + r, 4) * 8 + z, chip * 2 + (1 - core if other else core))
            part = x_buf.at[core, x]
            copy = remote(part, part, x_sem.at[0, 4 * other + r], x_sem.at[1, 4 * other + r], device)
            copy.start()
            steps.append(copy)
    for copy in steps:
        copy.wait_recv()
    for h in range(2):
        value = ((x_buf[h, 0] + x_buf[h, 1]) + x_buf[h, 2]) + x_buf[h, 3]
        sketch_ref[64:, 128 * h : 128 * h + 128] = value
    for item in sent + steps:
        item.wait_send()


def finish_kernel(sketch_ref, basis_ref, factor_ref):
    shape = (8, 128)
    lane = lanes(shape)
    sub = sublanes(shape)
    rows = []
    for i in range(8):
        at = 128 * (i // 4)
        block = sketch_ref[64 + 8 * (i % 2) : 72 + 8 * (i % 2), at : at + 128]
        if i % 4 >= 2:
            block = pltpu.roll(block, 64, 1)
        rows.append(jnp.where(lane < 64, block, jnp.where(lane - 64 == sub + 8 * i, 1.0, 0.0)))
    for n in range(8):
        columns = [[jnp.broadcast_to(rows[i][:, 8 * n + c : 8 * n + c + 1], shape) for i in range(n, 8)] for c in range(8)]
        own = rows[n]
        lines = []
        for c in range(8):
            pivot = jnp.broadcast_to(columns[c][0][c : c + 1, :], shape)
            scale = lax.rsqrt(pivot)
            line = jnp.broadcast_to(own[c : c + 1, :], shape) * scale
            columns[c] = [value * scale for value in columns[c]]
            below = jnp.where(sub > c, columns[c][0], 0.0)
            own = jnp.where(sub == c, line, own - below * line)
            for later in range(c + 1, 8):
                factor = jnp.broadcast_to(columns[c][0][later : later + 1, :], shape)
                columns[later][0] = columns[later][0] - below * factor
                for i in range(1, 8 - n):
                    columns[later][i] = columns[later][i] - columns[c][i] * factor
            lines.append(line)
        rows[n] = own
        for i in range(n + 1, 8):
            value = rows[i]
            for c in range(8):
                value = value - columns[c][i - n] * lines[c]
            rows[i] = value
    full = jnp.concatenate(rows, axis=0)
    row_at = lax.broadcasted_iota(jnp.int32, (64, 64), 0)
    col_at = lax.broadcasted_iota(jnp.int32, (64, 64), 1)
    upper = jnp.where(col_at >= row_at, full[:, :64], 0.0)
    factor_ref[...] = upper * (1.0 / math.sqrt(256))
    high, low = split2(full[:, 64:] * math.sqrt(256 * 128 * 64))
    left = jnp.concatenate([high, high, low], axis=1)
    for t in range(8):
        high, low = split2(sketch_ref[:64, 512 * t : 512 * t + 512])
        right = jnp.concatenate([high, low, high], axis=0)
        basis_ref[:, 512 * t : 512 * t + 512] = jnp.dot(left, right, preferred_element_type=F32)


def params(**more):
    return pltpu.CompilerParams(vmem_limit_bytes=48 * 1024 * 1024, **more)


def whole(space=VMEM):
    return pl.BlockSpec(memory_space=space)


def dma(*shape):
    return pltpu.SemaphoreType.DMA(shape)


def on_device(conductivity, leakage, signs, wells):
    cells = conductivity.shape[0] * conductivity.shape[1]
    probes = signs.shape[0] * GROUP
    count = wells.shape[0]
    wells = wells.reshape(1, count)

    def body(carry):
        turn, _, sketch = carry
        field = VMEM((SPAN, QUADS, 8, 128), F32)
        window = VMEM((SPAN, 2, QUADS, 8, 128), F32)
        sketch, rounds = pl.pallas_call(
            sketch_kernel,
            out_shape=(
                jax.ShapeDtypeStruct(sketch.shape, F32),
                jax.ShapeDtypeStruct((1,), jnp.int32),
            ),
            in_specs=[whole()] + [whole(pltpu.HBM)] * 4 + [whole()],
            out_specs=(whole(), whole(SMEM)),
            scratch_shapes=[
                VMEM((1, count), jnp.int32),
                VMEM(conductivity.shape, F32),
                VMEM(leakage.shape, F32),
                VMEM((64, 8, 128), F32),
                VMEM((64, 8, 128), F32),
                window,
                window,
                VMEM((2, CHIPS, probes // GROUP, count), jnp.int32),
                VMEM((7, SPAN, QUADS, 8, 128), F32),
                VMEM((2, SPAN, QUADS, 8, 128), F32),
                field,
                field,
                VMEM((SPAN, 8, QUADS, 128), F32),
                VMEM((SLOTS * QUADS, 128), F32),
                VMEM((256, 128), jnp.bfloat16),
                VMEM((2, probes, 128), F32),
                VMEM((2, 8, 128), F32),
                VMEM((SLOTS, 128), jnp.int32),
                VMEM((2, 16, 128), F32),
                VMEM((16, 128), F32),
                VMEM((8, 16, 128), F32),
                VMEM((8, 16, 128), F32),
                VMEM((2, 4, 16, 128), F32),
                dma(4),
                dma(2, 4),
                dma(2, 8),
                dma(2),
                dma(SPAN, 8),
                dma(SPAN, 8),
                dma(2, SPAN),
                dma(2),
                dma(2, 8),
                dma(2, 8),
                dma(2, 8),
            ],
            compiler_params=params(collective_id=0, has_side_effects=True),
            name="sketch",
        )(jnp.broadcast_to(turn, (1, count)), wells, conductivity, leakage, signs, sketch)
        return turn + 1, rounds[0], sketch

    sketch = jnp.zeros((probes + 16, cells // GROUP), F32)
    start = (jnp.int32(0), jnp.int32(1), sketch)
    _, _, sketch = lax.while_loop(lambda carry: carry[0] < carry[1], body, start)
    return pl.pallas_call(
        finish_kernel,
        out_shape=(
            jax.ShapeDtypeStruct((probes, cells // GROUP), F32),
            jax.ShapeDtypeStruct((probes, probes), F32),
        ),
        in_specs=[whole()],
        out_specs=(whole(), whole()),
        compiler_params=params(),
        name="finish",
    )(sketch)


def solution(mesh):
    placed = (P("space", None), P("space", None), P("probe", None), P())
    return jax.shard_map(
        on_device,
        mesh=mesh,
        in_specs=placed,
        out_specs=(P(None, ("space", "probe")), P()),
        check_vma=False,
    )
```

```python
import functools
import math

import jax
import jax.numpy as jnp
from jax import lax
from jax.experimental import pallas as pl
from jax.experimental.pallas import tpu as pltpu
from jax.sharding import PartitionSpec as P

NZ = 64
SWEEPS = 16
REACH = 2
SPAN = 2 * REACH + 1
GROUP = 16
CHIPS = 8
SLOTS = GROUP * SPAN
ORDER = (2, 1, 3, 0, 4)
EARLY = 3 * GROUP
LATE = SLOTS - EARLY
QUADS = 8
PAIRS = 32

bound_low = 0.005
bound_high = 24.5

F32 = jnp.float32
VMEM = pltpu.VMEM
SMEM = pltpu.SMEM


def chebyshev_table(count):
    center = 0.5 * (bound_high + bound_low)
    spread = 0.5 * (bound_high - bound_low)
    ratio = center / spread
    rho_prev = 1.0 / ratio
    entries = []
    for index_step in range(count):
        rho_next = 1.0 / (2.0 * ratio - rho_prev)
        entries.append((rho_next * rho_prev, 2.0 * rho_next / spread))
        rho_prev = rho_next
    return entries


def start_scale():
    return 1.0 / (0.5 * (bound_high + bound_low))


def decode(cell):
    cell = jnp.maximum(cell, 0)
    x = lax.shift_right_logical(cell, 13)
    y = lax.bitwise_and(lax.shift_right_logical(cell, 6), 127)
    z = lax.bitwise_and(cell, 63)
    y_first = lax.bitwise_and(y + 1, 126 + 128) - 16
    return x, y, y_first, z, z - 15


def lanes(shape=(8, 128)):
    return lax.broadcasted_iota(jnp.int32, shape, 1)


def sublanes(shape=(8, 128)):
    return lax.broadcasted_iota(jnp.int32, shape, 0)


def wrap(shift):
    return lax.bitwise_and(shift, 127)


OFFSETS = (-2, 2, -1, 1)


def barrier_with(partners):
    barrier = pltpu.get_barrier_semaphore()
    for partner in partners:
        pl.semaphore_signal(barrier, inc=1, device_id=partner, device_id_type=pl.DeviceIdType.MESH)
    return lambda: pl.semaphore_wait(barrier, len(partners))


def remote(src, dst, send, recv, device):
    return pltpu.make_async_remote_copy(
        src_ref=src, dst_ref=dst, send_sem=send, recv_sem=recv, device_id=device, device_id_type=pl.DeviceIdType.MESH
    )


def quads(block):
    return range(QUADS) if 0 < block < SPAN - 1 else range(2, 6)


def counted(owner, first, rows):
    shape = (rows, 256)
    lane = lanes(shape)
    ones = jnp.where(jnp.broadcast_to(owner, shape) == sublanes(shape) + first, 1, 0)
    total = ones
    for step in (1, 2, 4, 8, 16, 32, 64, 128):
        total = total + jnp.where(lane >= step, pltpu.roll(total, step, 1), 0)
    return ones, total - ones


def cut(cell, cell_row, e, cond_ref, leak_ref, out_ref):
    pair_first = lax.shift_right_arithmetic(decode(cell)[2], 1)
    shape = (256, 128)
    z_first = decode(jnp.broadcast_to(cell_row, shape))[4]
    row = sublanes(shape)
    lane = lanes(shape)
    same = lax.shift_right_logical(row, 6) == lax.shift_right_logical(lane, 5)
    hit = same & (lax.bitwise_and(row, 63) - z_first == lax.bitwise_and(lane, 31))
    move = jnp.where(hit, 1.0, 0.0).astype(jnp.bfloat16)
    parts = []
    for ref in (cond_ref, leak_ref):
        for k in quads(e):
            one = ref[jnp.clip(pair_first + 2 * k, 0, 63)]
            two = ref[jnp.clip(pair_first + 2 * k + 1, 0, 63)]
            parts.append(jnp.concatenate([one, two], axis=1))
    rows = 8 * len(parts)
    both = jnp.concatenate(split2(jnp.concatenate(parts, axis=0)), axis=0)
    both = jnp.dot(both, move, preferred_element_type=F32)
    both = both[:rows] + both[rows:]
    for n, k in enumerate(quads(e)):
        for prop in range(2):
            at = 8 * (n + prop * len(quads(e)))
            out_ref[e, prop, k] = both[at : at + 8]


def faces(cell, here, blocks, low, high, win_ref, coef):
    _, _, y_first, _, z_first = decode(cell)
    lane = lanes()
    sub = sublanes()
    group = lane // 32
    zz = z_first + lane % 32
    z_ok = (zz >= 0) & (zz < NZ)
    for b in blocks:
        xx = (here + (b - REACH)) * 8 + sub
        x_ok = (xx >= 0) & (xx < 256)
        for k in quads(b):
            yy = y_first + 4 * k + group
            inside = x_ok & (yy >= 0) & (yy < 128) & z_ok
            own = win_ref[b, 0, k]
            before = win_ref[max(b - 1, low), 0, k]
            after = win_ref[min(b + 1, high), 0, k]
            left = win_ref[b, 0, max(k - 1, 0)]
            right = win_ref[b, 0, min(k + 1, QUADS - 1)]
            parts = (
                (jnp.where(sub == 0, pltpu.roll(before, 1, 0), pltpu.roll(own, 1, 0)), xx >= 1),
                (jnp.where(sub == 7, pltpu.roll(after, 7, 0), pltpu.roll(own, 7, 0)), xx < 255),
                (jnp.where(group == 0, pltpu.roll(left, 32, 1), pltpu.roll(own, 32, 1)), yy >= 1),
                (jnp.where(group == 3, pltpu.roll(right, 96, 1), pltpu.roll(own, 96, 1)), yy < 127),
                (pltpu.roll(own, 1, 1), zz >= 1),
                (pltpu.roll(own, 127, 1), zz < NZ - 1),
            )
            diagonal = win_ref[b, 1, k]
            for n, (other, there) in enumerate(parts):
                face = 0.5 * (own + jnp.where(there, other, own))
                diagonal = diagonal + face
                coef[n + 1, b, k] = jnp.where(inside & there, face, 0.0)
            coef[0, b, k] = diagonal


def start_fields(cell, here, search, resid, total):
    x, y, y_first, _, _ = decode(cell)
    lane = lanes()
    sub = sublanes()
    weight = jnp.where(cell >= 0, 1.0, 0.0).astype(F32)
    zero = jnp.zeros((8, 128), F32)
    for b in range(SPAN):
        for k in range(QUADS):
            search[1, b, k] = zero
            if b == REACH and k in (3, 4):
                hit = (sub == x - here * 8) & (4 * k + lane // 32 == y - y_first) & (lane % 32 == 15)
                source = jnp.where(hit, weight, 0.0)
                resid[b, k] = source
                search[0, b, k] = source * start_scale()
            else:
                resid[b, k] = zero
                search[0, b, k] = zero
            total[b, k] = zero


def sweeps(steps, coef, search, resid, total):
    group = lanes() // 32
    sub = sublanes()
    zero = jnp.zeros((8, 128), F32)
    table = chebyshev_table(SWEEPS)
    for j in steps:
        a, c = (float(value) for value in table[j])
        now, later = j % 2, (j + 1) % 2
        wide = j + 1
        k_low, k_high = (15 - wide) // 4, (16 + wide) // 4
        b_low, b_high = (1, 3) if wide <= 8 else (0, 4)
        for b in range(b_low, b_high + 1):
            for k in range(max(k_low, quads(b)[0]), min(k_high, quads(b)[-1]) + 1):
                own = search[now, b, k]
                edge = pltpu.roll(search[now, b - 1, k], 1, 0) if b > 0 else zero
                down = jnp.where(sub == 0, edge, pltpu.roll(own, 1, 0))
                edge = pltpu.roll(search[now, b + 1, k], 7, 0) if b < SPAN - 1 else zero
                up = jnp.where(sub == 7, edge, pltpu.roll(own, 7, 0))
                edge = pltpu.roll(search[now, b, k - 1], 32, 1) if k > 0 else zero
                left = jnp.where(group == 0, edge, pltpu.roll(own, 32, 1))
                edge = pltpu.roll(search[now, b, k + 1], 96, 1) if k < QUADS - 1 else zero
                right = jnp.where(group == 3, edge, pltpu.roll(own, 96, 1))
                image = coef[0, b, k] * own
                image = image - coef[1, b, k] * down
                image = image - coef[2, b, k] * up
                image = image - coef[3, b, k] * left
                image = image - coef[4, b, k] * right
                image = image - coef[5, b, k] * pltpu.roll(own, 1, 1)
                image = image - coef[6, b, k] * pltpu.roll(own, 127, 1)
                rest = resid[b, k] - image
                resid[b, k] = rest
                total[b, k] = total[b, k] + own
                search[later, b, k] = a * own + c * rest


def split2(value):
    high = value.astype(jnp.bfloat16)
    return high, (value - high.astype(F32)).astype(jnp.bfloat16)


def moves(cell):
    shape = (256, 128)
    _, _, y_first, _, z_first = decode(jnp.broadcast_to(cell[0:1, :], shape))
    lane = lanes(shape)
    row = sublanes(shape)
    odd = lax.bitwise_and(lax.shift_right_arithmetic(y_first, 1), 1)
    same_z = lax.bitwise_and(row + z_first, 31) == lax.bitwise_and(lane, 31)
    same_y = lax.bitwise_and(lax.shift_right_logical(row, 5) + 2 * odd, 3) == lax.shift_right_logical(lane, 5)
    hit = same_z & same_y & ((row < 128) == (lane < 64))
    return jnp.where(hit, 1.0, 0.0).astype(jnp.bfloat16)


def align(first, second, b, move, total, out_ref):
    one = split2(jnp.concatenate([total[b, lax.bitwise_and(k - first, 7)] for k in range(QUADS)], axis=0))
    two = split2(jnp.concatenate([total[b, lax.bitwise_and(k - second, 7)] for k in range(QUADS)], axis=0))
    both = jnp.concatenate([jnp.concatenate(part, axis=1) for part in zip(one, two)], axis=0)
    both = jnp.dot(both, move[...], preferred_element_type=F32)
    both = both[:64] + both[64:]
    for k in range(QUADS):
        out_ref[b, :, k, :] = both[8 * k : 8 * k + 8]


def slots(ones, counts, wells, turn, chip):
    shape = (GROUP, 256)
    place = sublanes(shape)
    probe = 2 * lax.bitwise_and(chip - lax.bitwise_and(place, 7), 7) + lax.shift_right_logical(place, 3)
    want = probe + GROUP * jnp.broadcast_to(turn, shape)
    parts = []
    for e in ORDER:
        there = jnp.broadcast_to(ones[e : e + 1], shape) > 0
        parts.append(there & (jnp.broadcast_to(counts[e : e + 1], shape) == want))
    holds = [jnp.where(part, 1.0, 0.0) for part in parts]
    wells = jnp.broadcast_to(wells, shape)
    cells = [jnp.max(jnp.where(part, wells, -1), axis=1, keepdims=True) for part in parts]
    return jnp.concatenate(holds, axis=0), jnp.concatenate(cells, axis=0)


def align_far(first, second, b, move, total, out_ref, at):
    one = split2(jnp.concatenate([total[b, 2 + lax.bitwise_and(k - first - 2, 3)] for k in range(4)], axis=0))
    two = split2(jnp.concatenate([total[b, 2 + lax.bitwise_and(k - second - 2, 3)] for k in range(4)], axis=0))
    both = jnp.concatenate([jnp.concatenate(part, axis=1) for part in zip(one, two)], axis=0)
    both = jnp.dot(both, move[...], preferred_element_type=F32)
    both = both[:32] + both[32:]
    for k in range(4):
        out_ref[at, :, k, :] = both[8 * k : 8 * k + 8]


def panel(pick, pair_first, z_first, half, load, quads_here, add):
    number = z_first.shape[0]
    width = 2 * quads_here
    pair_first = pair_first - float(PAIRS) * half.astype(F32) + float(8 - quads_here)
    lane = lanes((number, 128))
    z_here = lane % 64 - z_first
    shown = (z_here >= 0) & (z_here < 32)
    group = lane // 32
    rest = 64 - number
    for k in range(quads_here):
        own = load(k)
        r1, r2, r3 = (pltpu.roll(own, 32 * n, 1) for n in (1, 2, 3))
        pairs = (
            jnp.where(group == 0, own, jnp.where(group == 3, r2, r1)),
            jnp.where(group == 0, r2, jnp.where(group == 3, own, r3)),
        )
        for m in range(2):
            high, low = split2(jnp.where(shown, pairs[m], 0.0))
            blank = jnp.zeros((rest, 128), jnp.bfloat16)
            value = jnp.concatenate([high, blank, low, blank], axis=0)
            places = range(2 * k + m, PAIRS, width)
            left = []
            for t in places:
                ok = (pair_first <= t) & (t < pair_first + width)
                left.append(jnp.where(ok, pick, 0.0).astype(jnp.bfloat16))
            both = jnp.dot(jnp.concatenate(left, axis=0), value, preferred_element_type=F32)
            for n, t in enumerate(places):
                add(128 * t, both[64 * n : 64 * n + 64])


def doubled(value, first, number):
    lane = lanes(value.shape)
    low = pltpu.roll(value, (128 - first) % 128, 1) if first else value
    return jnp.where(lane % 64 < number, jnp.where(lane < 64, low, pltpu.roll(value, (192 - first) % 128, 1)), 0.0)


def gram_of(sketch_ref):
    both = jnp.concatenate(split2(sketch_ref[:64, :]), axis=0)
    full = lax.dot_general(both, both, (((1,), (1,)), ((), ())), preferred_element_type=F32)
    return full[:64, :64] + ((full[:64, 64:] + full[64:, :64]) + full[64:, 64:])


def sketch_kernel(
    turn_ref,
    wells_hbm,
    cond_hbm,
    leak_hbm,
    signs_hbm,
    before_ref,
    sketch_ref,
    rounds_ref,
    wells_ref,
    cond_ref,
    leak_ref,
    cond_pairs,
    leak_pairs,
    cuts,
    win,
    signs,
    coef,
    search,
    resid,
    total,
    fields,
    far_fields,
    rows,
    far_rows,
    move,
    pick_ref,
    first_ref,
    depth_ref,
    mine,
    twin_buf,
    y_buf,
    z_buf,
    x_buf,
    load_sem,
    win_sem,
    sign_sem,
    sign_pair,
    row_send,
    row_recv,
    pair_sem,
    twin_sem,
    y_sem,
    z_sem,
    x_sem,
):
    count = lax.axis_size("space")
    here = lax.axis_index("space")
    me = lax.axis_index("probe")
    chip = me // 2
    core = me % 2
    x = here // 8
    z = here % 8
    near = [(lax.rem(here + d + count, count), me) for d in OFFSETS]
    along = [(here, lax.rem(chip + r, CHIPS) * 2 + core) for r in range(1, CHIPS)]
    ring_z = [(x * 8 + lax.rem(z + r, 8), me) for r in range(1, 8)]
    ring_x = [(lax.rem(x + r, 4) * 8 + z, me) for r in range(1, 4)]
    twin = (here, chip * 2 + 1 - core)
    entered = barrier_with(near + along + [twin] + ring_z + ring_x)
    loads = []
    pieces = ((wells_hbm, wells_ref), (cond_hbm, cond_ref), (leak_hbm, leak_ref), (signs_hbm, signs.at[core, chip]))
    for i, (src, dst) in enumerate(pieces):
        loads.append(pltpu.make_async_copy(src, dst, load_sem.at[i]))
        loads[-1].start()
    one = jnp.ones((8, 128), F32)
    for b in (0, SPAN - 1):
        for k in range(QUADS):
            if k not in quads(b):
                win[b, 0, k] = one
    loads[0].wait()
    wells = wells_ref[...]
    turn = turn_ref[...]
    owner = lax.shift_right_logical(wells, 16)
    ones, counts = counted(owner, here - REACH, 8)
    chosen = (ones > 0) & (counts == me + GROUP * jnp.broadcast_to(turn, (8, 256)))
    cells = jnp.max(jnp.where(chosen, jnp.broadcast_to(wells, (8, 256)), -1), axis=1, keepdims=True)
    cell = jnp.broadcast_to(cells[REACH : REACH + 1], (8, 128))
    for copy in loads[1:]:
        copy.wait()
    for src, dst in ((cond_ref, cond_pairs), (leak_ref, leak_pairs)):
        for t in range(64):
            dst[t] = src[:, 128 * t : 128 * t + 128]
    for e in range(SPAN):
        cut(cells[e, 0], cells[e : e + 1], e, cond_pairs, leak_pairs, cuts)
    entered()
    sent = []
    windows = []
    for i, d in enumerate(OFFSETS):
        src, dst = cuts.at[d + 2], win.at[2 - d]
        if d in (-2, 2):
            src, dst = cuts.at[d + 2, :, pl.ds(2, 4)], win.at[2 - d, :, pl.ds(2, 4)]
        copy = remote(src, dst, win_sem.at[0, i], win_sem.at[1, i], near[i])
        copy.start()
        windows.append(copy)
    win[REACH] = cuts[REACH]
    start_fields(cell, here, search, resid, total)
    move[...] = moves(cell)
    all_ones, all_counts = counted(owner, 0, count)
    rounds_ref[0] = lax.shift_right_logical(jnp.max(jnp.where(all_ones > 0, all_counts, 0)), 4) + 1
    holds, slot_cells = slots(ones, counts, wells, turn, chip)
    _, _, y_first, _, z_first = decode(jnp.broadcast_to(slot_cells, (SLOTS, 128)))
    depth_ref[...] = z_first
    pairs_first = lax.shift_right_arithmetic(y_first, 1).astype(F32)
    pairs_first = jnp.concatenate([pairs_first, jnp.zeros((128 - SLOTS, 128), F32)], axis=0)
    pairs_first = pairs_first.T
    for copy in windows[2:]:
        copy.wait_recv()
    shared = []
    for r in range(1, CHIPS):
        part = signs.at[core, chip]
        copy = remote(part, part, sign_sem.at[0, r], sign_sem.at[1, r], along[r - 1])
        copy.start()
        shared.append(copy)
    faces(cell, here, (1, 2, 3), 1, 3, win, coef)
    sweeps(range(8), coef, search, resid, total)
    for copy in windows[:2]:
        copy.wait_recv()
    faces(cell, here, (0, 1, 3, 4), 0, 4, win, coef)
    sweeps(range(8, SWEEPS - 1), coef, search, resid, total)
    last = (SWEEPS - 1) % 2
    for b in range(SPAN):
        for k in range(QUADS):
            total[b, k] = total[b, k] + search[last, b, k]
    y_first = decode(cells[REACH, 0])[2]
    second = lax.shift_right_arithmetic(y_first, 2)
    first = second + lax.bitwise_and(lax.shift_right_arithmetic(y_first, 1), 1)
    arrivals = {}
    for d in OFFSETS + (0,):
        far = d in (-2, 2)
        if far:
            align_far(first, second, d + 2, move, total, far_fields, (d + 2) // 4)
        else:
            align(first, second, d + 2, move, total, fields)
        e = 2 - d
        for r in (4, 3, 5, 2, 6, 1, 7, 0):
            target = lax.rem(chip + r, CHIPS)
            if far:
                source = far_fields.at[(d + 2) // 4, target]
                place = far_rows.at[(ORDER.index(e) - 3) * GROUP + core * CHIPS + r]
            else:
                source = fields.at[d + 2, target]
                place = rows.at[pl.ds(pl.multiple_of((ORDER.index(e) * GROUP + core * CHIPS + r) * 8, 8), 8)]
            if d == 0 and r == 0:
                rows[pl.ds(pl.multiple_of((ORDER.index(e) * GROUP + core * CHIPS) * 8, 8), 8), :] = fields[REACH, chip]
                continue
            device = (lax.rem(here + d + count, count), target * 2 + core)
            copy = remote(source, place, row_send.at[d + 2, r], row_recv.at[e, r], device)
            copy.start()
            arrivals[e, r] = copy
    for copy in shared:
        copy.wait_recv()
    pair = remote(signs.at[core], signs.at[core], sign_pair.at[0], sign_pair.at[1], twin)
    pair.start()
    pair.wait_recv()
    table = jnp.concatenate([signs[p % 2, p // 2] for p in range(GROUP)], axis=0)
    table = (2 * table - 1).astype(F32).astype(jnp.bfloat16)
    holds = jnp.concatenate([holds, jnp.zeros((128 - SLOTS, 256), F32)], axis=0).astype(jnp.bfloat16)
    pick = lax.dot_general(table, holds, (((1,), (1,)), ((), ())), preferred_element_type=F32)
    keep = jnp.where(turn[:, :128] > 0, 1.0, 0.0)
    parts = ((0, EARLY), (EARLY, LATE))
    for n, (start, number) in enumerate(parts):
        pick_ref[n] = doubled(pick, start, number)
        first_ref[n] = doubled(pairs_first[0:8], start, number)

    def put(at, value):
        sketch_ref[:64, at : at + 128] = value + keep * before_ref[:64, at : at + 128]

    def add(at, value):
        sketch_ref[:64, at : at + 128] = sketch_ref[:64, at : at + 128] + value

    pairs = []
    for e in ORDER:
        for r in range(CHIPS):
            if (e, r) != (REACH, 0):
                arrivals[e, r].wait_recv()
        if e in (0, SPAN - 1):
            part = far_rows.at[pl.ds((ORDER.index(e) - 3) * GROUP + core * CHIPS, CHIPS)]
        else:
            part = rows.at[pl.ds(pl.multiple_of((ORDER.index(e) * GROUP + core * CHIPS) * 8, 8), 8 * CHIPS)]
        copy = remote(part, part, pair_sem.at[0, e], pair_sem.at[1, e], twin)
        copy.start()
        pairs.append(copy)
        if e == 3:
            for copy in pairs:
                copy.wait_recv()
            panel(
                pick_ref[0],
                first_ref[0, 0:1, :],
                depth_ref[:EARLY, :],
                core,
                lambda k: rows[pl.ds(k, EARLY, stride=8), :],
                QUADS,
                put,
            )
    for copy in pairs[3:]:
        copy.wait_recv()
    panel(pick_ref[1], first_ref[1, 0:1, :], depth_ref[EARLY:, :], core, lambda k: far_rows[:, k, :], 4, add)
    sent += windows + shared + [pair] + list(arrivals.values()) + pairs
    gram = gram_of(sketch_ref)
    for h in range(2):
        mine[h] = jnp.concatenate([gram[32 * h : 32 * h + 16], gram[32 * h + 16 : 32 * h + 32]], axis=1)
    copy = remote(mine.at[1 - core], twin_buf, twin_sem.at[0], twin_sem.at[1], twin)
    copy.start()
    sent.append(copy)
    copy.wait_recv()
    value = mine[core] + twin_buf[...]
    for buf, sem, at, ring in ((y_buf, y_sem, chip, along), (z_buf, z_sem, z, ring_z)):
        buf[at] = value
        steps = []
        for r, device in sorted(enumerate(ring), key=lambda item: abs(2 * item[0] + 1 - len(ring))):
            copy = remote(buf.at[at], buf.at[at], sem.at[0, r], sem.at[1, r], device)
            copy.start()
            steps.append(copy)
        for copy in steps:
            copy.wait_recv()
        sent += steps
        value = buf[0]
        for r in range(1, 8):
            value = value + buf[r]
    x_buf[core, x] = value
    steps = []
    for r in (2, 1, 3, 0):
        for other in range(2):
            if r == 0 and other == 0:
                continue
            device = (lax.rem(x + r, 4) * 8 + z, chip * 2 + (1 - core if other else core))
            part = x_buf.at[core, x]
            copy = remote(part, part, x_sem.at[0, 4 * other + r], x_sem.at[1, 4 * other + r], device)
            copy.start()
            steps.append(copy)
    for copy in steps:
        copy.wait_recv()
    for h in range(2):
        value = ((x_buf[h, 0] + x_buf[h, 1]) + x_buf[h, 2]) + x_buf[h, 3]
        sketch_ref[64:, 128 * h : 128 * h + 128] = value
    for item in sent + steps:
        item.wait_send()


def finish_kernel(sketch_ref, basis_ref, factor_ref):
    shape = (8, 128)
    lane = lanes(shape)
    sub = sublanes(shape)
    rows = []
    for i in range(8):
        at = 128 * (i // 4)
        block = sketch_ref[64 + 8 * (i % 2) : 72 + 8 * (i % 2), at : at + 128]
        if i % 4 >= 2:
            block = pltpu.roll(block, 64, 1)
        rows.append(jnp.where(lane < 64, block, jnp.where(lane - 64 == sub + 8 * i, 1.0, 0.0)))
    for n in range(8):
        columns = [[jnp.broadcast_to(rows[i][:, 8 * n + c : 8 * n + c + 1], shape) for i in range(n, 8)] for c in range(8)]
        own = rows[n]
        lines = []
        for c in range(8):
            pivot = jnp.broadcast_to(columns[c][0][c : c + 1, :], shape)
            scale = lax.rsqrt(pivot)
            line = jnp.broadcast_to(own[c : c + 1, :], shape) * scale
            columns[c] = [value * scale for value in columns[c]]
            below = jnp.where(sub > c, columns[c][0], 0.0)
            own = jnp.where(sub == c, line, own - below * line)
            for later in range(c + 1, 8):
                factor = jnp.broadcast_to(columns[c][0][later : later + 1, :], shape)
                columns[later][0] = columns[later][0] - below * factor
                for i in range(1, 8 - n):
                    columns[later][i] = columns[later][i] - columns[c][i] * factor
            lines.append(line)
        rows[n] = own
        for i in range(n + 1, 8):
            value = rows[i]
            for c in range(8):
                value = value - columns[c][i - n] * lines[c]
            rows[i] = value
    full = jnp.concatenate(rows, axis=0)
    row_at = lax.broadcasted_iota(jnp.int32, (64, 64), 0)
    col_at = lax.broadcasted_iota(jnp.int32, (64, 64), 1)
    upper = jnp.where(col_at >= row_at, full[:, :64], 0.0)
    factor_ref[...] = upper * (1.0 / math.sqrt(256))
    high, low = split2(full[:, 64:] * math.sqrt(256 * 128 * 64))
    left = jnp.concatenate([high, high, low], axis=1)
    for t in range(8):
        high, low = split2(sketch_ref[:64, 512 * t : 512 * t + 512])
        right = jnp.concatenate([high, low, high], axis=0)
        basis_ref[:, 512 * t : 512 * t + 512] = jnp.dot(left, right, preferred_element_type=F32)


def params(**more):
    return pltpu.CompilerParams(vmem_limit_bytes=48 * 1024 * 1024, **more)


def whole(space=VMEM):
    return pl.BlockSpec(memory_space=space)


def dma(*shape):
    return pltpu.SemaphoreType.DMA(shape)


def on_device(conductivity, leakage, signs, wells):
    cells = conductivity.shape[0] * conductivity.shape[1]
    probes = signs.shape[0] * GROUP
    count = wells.shape[0]
    wells = wells.reshape(1, count)

    def body(carry):
        turn, _, sketch = carry
        field = VMEM((SPAN, QUADS, 8, 128), F32)
        window = VMEM((SPAN, 2, QUADS, 8, 128), F32)
        sketch, rounds = pl.pallas_call(
            sketch_kernel,
            out_shape=(
                jax.ShapeDtypeStruct(sketch.shape, F32),
                jax.ShapeDtypeStruct((1,), jnp.int32),
            ),
            in_specs=[whole()] + [whole(pltpu.HBM)] * 4 + [whole()],
            out_specs=(whole(), whole(SMEM)),
            scratch_shapes=[
                VMEM((1, count), jnp.int32),
                VMEM(conductivity.shape, F32),
                VMEM(leakage.shape, F32),
                VMEM((64, 8, 128), F32),
                VMEM((64, 8, 128), F32),
                window,
                window,
                VMEM((2, CHIPS, probes // GROUP, count), jnp.int32),
                VMEM((7, SPAN, QUADS, 8, 128), F32),
                VMEM((2, SPAN, QUADS, 8, 128), F32),
                field,
                field,
                VMEM((SPAN, 8, QUADS, 128), F32),
                VMEM((2, 8, 4, 128), F32),
                VMEM((EARLY * QUADS, 128), F32),
                VMEM((LATE, 4, 128), F32),
                VMEM((256, 128), jnp.bfloat16),
                VMEM((2, probes, 128), F32),
                VMEM((2, 8, 128), F32),
                VMEM((SLOTS, 128), jnp.int32),
                VMEM((2, 16, 128), F32),
                VMEM((16, 128), F32),
                VMEM((8, 16, 128), F32),
                VMEM((8, 16, 128), F32),
                VMEM((2, 4, 16, 128), F32),
                dma(4),
                dma(2, 4),
                dma(2, 8),
                dma(2),
                dma(SPAN, 8),
                dma(SPAN, 8),
                dma(2, SPAN),
                dma(2),
                dma(2, 8),
                dma(2, 8),
                dma(2, 8),
            ],
            compiler_params=params(collective_id=0, has_side_effects=True),
            name="sketch",
        )(jnp.broadcast_to(turn, (1, count)), wells, conductivity, leakage, signs, sketch)
        return turn + 1, rounds[0], sketch

    sketch = jnp.zeros((probes + 16, cells // GROUP), F32)
    start = (jnp.int32(0), jnp.int32(1), sketch)
    _, _, sketch = lax.while_loop(lambda carry: carry[0] < carry[1], body, start)
    return pl.pallas_call(
        finish_kernel,
        out_shape=(
            jax.ShapeDtypeStruct((probes, cells // GROUP), F32),
            jax.ShapeDtypeStruct((probes, probes), F32),
        ),
        in_specs=[whole()],
        out_specs=(whole(), whole()),
        compiler_params=params(),
        name="finish",
    )(sketch)


def solution(mesh):
    placed = (P("space", None), P("space", None), P("probe", None), P())
    return jax.shard_map(
        on_device,
        mesh=mesh,
        in_specs=placed,
        out_specs=(P(None, ("space", "probe")), P()),
        check_vma=False,
    )
```
